32 devices in a mesh: lon: 8 (over y, x, core), rep: 4 (over z).
Axes of the slice: x: 2, y: 2, z: 4, core: 2. Of those that a mesh axis runs over, the one named last changes fastest.
Arguments:
- fields: bfloat16 [32, 24, 64, 256], P('rep', None, 'lon'), may hold values from -6 to 6
- stem_weight: bfloat16 [32, 24, 4, 4], replicated, may hold values from -0.3125 to 0.3125
- mid_weight: bfloat16 [64, 32, 3, 3], replicated, may hold values from -0.375 to 0.375
- head_weight: bfloat16 [64, 64, 3, 3], replicated, may hold values from -0.25 to 0.25
- out_weight: float32 [64], replicated, may hold values from -0.75 to 0.75
- pred_cotangent: float32 [32, 16, 64], P(('rep', 'lon')), may hold values from -6 to 6
Outputs:
- prediction: float32 [32, 16, 64], P(('rep', 'lon'))
- stem_cotangent: bfloat16 [32, 32, 32, 128], P('rep', None, 'lon')
- grad_stem: float32 [32, 24, 4, 4], replicated
- grad_mid: float32 [64, 32, 3, 3], replicated
- grad_head: float32 [64, 64, 3, 3], replicated
- grad_out: float32 [64], replicated
The draws below stay inside these ranges and needn't reach their ends.
All inputs are finite; a program needn't handle non-finite values.
Results may differ from the reference program's by a relative error of at most 0.0085.
Values may be sent and summed in bfloat16 or wider, within the bound.
A program may use at most 128 MiB of HBM per device.

```python
import jax
import jax.numpy as jnp
from jax import lax

C_IN = 24
C1 = 32
C2 = 64
LAT = 256
SCEN = 32
LON = 64
LONH = 32
LATH = 128
LONC = 16
LATC = 64


def steps_of(stream_key, dims, shards, smallest, top_value):
    def one(axis_at, parts):
        draws = jax.random.uniform(jax.random.fold_in(jax.random.fold_in(stream_key, 6), axis_at), (parts,), jnp.float32, smallest / len(shards), top_value / len(shards))
        return jnp.repeat(jnp.exp(draws), dims[axis_at] // parts).reshape((-1,) + (1,) * (len(dims) - axis_at - 1))

    factor_of = one(*shards[0])
    for cut in shards[1:]:
        factor_of = factor_of * one(*cut)
    return factor_of


def gaussian(key, dims, scale, reach, cuts=(), held_as=jnp.bfloat16):
    loudness = steps_of(key, dims, cuts, -0.22, 0.18) if cuts else 1.0
    drawn = jax.random.normal(key, dims, jnp.float32) * scale * loudness
    return jnp.minimum(jnp.maximum(drawn, -reach), reach).astype(held_as)


def setup_inputs(seed: int = 0) -> dict:
    streams_of = jax.random.split(jax.random.key(seed), 7)
    return {
        "fields": gaussian(streams_of[0], (SCEN, C_IN, LON, LAT), 1.0, 6.0, ((0, 4), (2, 8))),
        "stem_weight": gaussian(streams_of[1], (C1, C_IN, 4, 4), (C_IN * 16) ** -0.5, 0.3125),
        "mid_weight": gaussian(streams_of[2], (C2, C1, 3, 3), (C1 * 9) ** -0.5, 0.375),
        "head_weight": gaussian(streams_of[3], (C2, C2, 3, 3), (C2 * 9) ** -0.5, 0.25),
        "out_weight": gaussian(streams_of[4], (C2,), C2 ** -0.5, 0.75, (), jnp.float32),
        "pred_cotangent": gaussian(streams_of[5], (SCEN, LONC, LATC), 1.0, 6.0, ((0, 32),), jnp.float32),
    }


exact_mode = lax.Precision.HIGHEST

def window(padded, tap_row, tap_col, out_rows, out_cols, stride):
    upper_corner = (padded.shape[0], padded.shape[1], tap_row + stride * (out_rows - 1) + 1, tap_col + stride * (out_cols - 1) + 1)
    return lax.slice(padded, (0, 0, tap_row, tap_col), upper_corner, (1, 1, stride, stride))

def conv_forward(padded, weight, stride, out_rows, out_cols):
    summed = None
    for tap_row in range(weight.shape[2]):
        for tap_col in range(weight.shape[3]):
            inputs = window(padded, tap_row, tap_col, out_rows, out_cols, stride)
            partial_term = jnp.einsum('sihw,oi->sohw', inputs, weight[:, :, tap_row, tap_col], precision=exact_mode)
            summed = partial_term if summed is None else summed + partial_term
    return summed

def conv_weight_grad(padded, cotangent, kernel, stride):
    out_rows, out_cols = (cotangent.shape[2], cotangent.shape[3])
    stacked_rows = []
    for tap_row in range(kernel):
        across = []
        for tap_col in range(kernel):
            inputs = window(padded, tap_row, tap_col, out_rows, out_cols, stride)
            across.append(jnp.einsum('sohw,sihw->oi', cotangent, inputs, precision=exact_mode))
        stacked_rows.append(jnp.stack(across, 2))
    return jnp.stack(stacked_rows, 2)

def conv_input_grad(cotangent, weight, stride, padded_shape):
    out_rows, out_cols = (cotangent.shape[2], cotangent.shape[3])
    gradient = jnp.zeros(padded_shape, jnp.float32)
    for tap_row in range(weight.shape[2]):
        for tap_col in range(weight.shape[3]):
            spread = jnp.einsum('sohw,oi->sihw', cotangent, weight[:, :, tap_row, tap_col], precision=exact_mode)
            gradient = gradient.at[:, :, tap_row:tap_row + stride * (out_rows - 1) + 1:stride, tap_col:tap_col + stride * (out_cols - 1) + 1:stride].add(spread)
    return gradient

def slope(values):
    sigma = jax.nn.sigmoid(values)
    return sigma * (1.0 + values * (1.0 - sigma))

def lat_pad(field, before, after):
    return jnp.pad(field, ((0, 0), (0, 0), (0, 0), (before, after)))

def to_half(values):
    return lax.optimization_barrier(values.astype(jnp.bfloat16))

def reference(fields, stem_weight, mid_weight, head_weight, out_weight, pred_cotangent):
    stem_full = stem_weight.astype(jnp.float32)
    mid_full = mid_weight.astype(jnp.float32)
    head_full = head_weight.astype(jnp.float32)

    def one_scenario(totals, inputs):
        field_one, cot_one = inputs
        field_one = field_one[None].astype(jnp.float32)
        cot_one = cot_one[None]
        padded_fields = lat_pad(jnp.concatenate([field_one[:, :, -1:], field_one, field_one[:, :, :1]], 2), 1, 1)
        stem_pre = conv_forward(padded_fields, stem_full, 2, LONH, LATH)
        stem_act = to_half(jax.nn.silu(stem_pre)).astype(jnp.float32)
        mid_padded = lat_pad(jnp.concatenate([stem_act[:, :, -1:], stem_act], 2), 1, 0)
        mid_pre = conv_forward(mid_padded, mid_full, 2, LONC, LATC)
        mid_act = to_half(jax.nn.silu(mid_pre)).astype(jnp.float32)
        head_padded = lat_pad(jnp.concatenate([mid_act[:, :, -1:], mid_act, mid_act[:, :, :1]], 2), 1, 1)
        head_pre = conv_forward(head_padded, head_full, 1, LONC, LATC)
        head_act = to_half(jax.nn.silu(head_pre)).astype(jnp.float32)
        prediction = jnp.einsum('c,schw->shw', out_weight, head_act, precision=exact_mode)
        head_cot = to_half(cot_one[:, None] * out_weight[None, :, None, None] * slope(head_pre)).astype(jnp.float32)
        out_sum = jnp.einsum('shw,schw->c', cot_one, head_act, precision=exact_mode)
        head_sum = conv_weight_grad(head_padded, head_cot, 3, 1)
        head_spread = conv_input_grad(head_cot, head_full, 1, head_padded.shape)
        mid_grad = head_spread[:, :, 1:-1, 1:-1]
        mid_grad = mid_grad.at[:, :, -1].add(head_spread[:, :, 0, 1:-1]).at[:, :, 0].add(head_spread[:, :, -1, 1:-1])
        mid_grad = to_half(mid_grad).astype(jnp.float32)
        mid_cot = to_half(mid_grad * slope(mid_pre)).astype(jnp.float32)
        mid_sum = conv_weight_grad(mid_padded, mid_cot, 3, 2)
        mid_spread = conv_input_grad(mid_cot, mid_full, 2, mid_padded.shape)
        stem_grad = mid_spread[:, :, 1:, 1:].at[:, :, -1].add(mid_spread[:, :, 0, 1:])
        stem_grad = to_half(stem_grad).astype(jnp.float32)
        stem_cot = (stem_grad * slope(stem_pre)).astype(jnp.bfloat16)
        stem_sum = conv_weight_grad(padded_fields, stem_cot.astype(jnp.float32), 4, 2)
        new_totals = (totals[0] + stem_sum, totals[1] + mid_sum, totals[2] + head_sum, totals[3] + out_sum)
        return (new_totals, (prediction[0], stem_cot[0]))
    initial = (jnp.zeros((C1, C_IN, 4, 4), jnp.float32), jnp.zeros((C2, C1, 3, 3), jnp.float32), jnp.zeros((C2, C2, 3, 3), jnp.float32), jnp.zeros((C2,), jnp.float32))
    totals, (prediction, stem_cotangent) = lax.scan(one_scenario, initial, (fields, pred_cotangent))
    factor = 1.0 / SCEN
    return (prediction, stem_cotangent, totals[0] * factor, totals[1] * factor, totals[2] * factor, totals[3] * factor)
```

```python
import functools

import jax
import jax.numpy as jnp
from jax import lax
from jax.experimental import pallas as pl
from jax.experimental.pallas import tpu as pltpu
from jax.sharding import PartitionSpec as P


MESH = pl.DeviceIdType.MESH


def total_kernel(nl, nr, x_ref, out_ref, half, got1, mine, got2, got3, s1, r1, s2, r2, s3, r3):
    rows = x_ref.shape[0] // nl
    me, rep = lax.axis_index("lon"), lax.axis_index("rep")

    def lon_peer(k):
        return (lax.rem(me + k, nl), rep)

    def rep_peer(k):
        return (me, lax.rem(rep + k, nr))

    barrier = pltpu.get_barrier_semaphore()
    for k in range(1, nl):
        pl.semaphore_signal(barrier, inc=1, device_id=lon_peer(k), device_id_type=MESH)
    for k in range(1, nr):
        pl.semaphore_signal(barrier, inc=1, device_id=rep_peer(k), device_id_type=MESH)
    half[...] = x_ref[...].astype(jnp.bfloat16)
    pl.semaphore_wait(barrier, nl - 1 + nr - 1)

    def part(at):
        return pl.ds(pl.multiple_of(at * rows, rows), rows)

    first = []
    for k in range(1, nl):
        copy = pltpu.make_async_remote_copy(
            src_ref=half.at[part(lax.rem(me + k, nl))],
            dst_ref=got1.at[k - 1],
            send_sem=s1.at[k - 1],
            recv_sem=r1.at[k - 1],
            device_id=lon_peer(k),
            device_id_type=MESH,
        )
        copy.start()
        first.append(copy)
    total = x_ref[part(me), :]
    for k in range(1, nl):
        first[k - 1].wait_recv()
        total = total + got1[k - 1].astype(jnp.float32)
    mine[...] = total.astype(jnp.bfloat16)
    second = []
    for k in range(1, nr):
        copy = pltpu.make_async_remote_copy(
            src_ref=mine,
            dst_ref=got2.at[rep],
            send_sem=s2.at[k - 1],
            recv_sem=r2.at[k - 1],
            device_id=rep_peer(k),
            device_id_type=MESH,
        )
        copy.start()
        second.append(copy)
    got2[rep] = mine[...]
    for copy in second:
        copy.wait_recv()
    total = got2[0].astype(jnp.float32)
    for k in range(1, nr):
        total = total + got2[k].astype(jnp.float32)
    got3[part(me), :] = total.astype(jnp.bfloat16)
    third = []
    for k in range(1, nl):
        copy = pltpu.make_async_remote_copy(
            src_ref=got3.at[part(me)],
            dst_ref=got3.at[part(me)],
            send_sem=s3.at[k - 1],
            recv_sem=r3.at[k - 1],
            device_id=lon_peer(k),
            device_id_type=MESH,
        )
        copy.start()
        third.append(copy)
    for copy in third:
        copy.wait_recv()
    out_ref[...] = got3[...].astype(jnp.float32)
    for copy in first + second + third:
        copy.wait_send()


def total_over_all(x, nl, nr):
    rows = x.shape[0] // nl
    dma = pltpu.SemaphoreType.DMA
    vmem = pl.BlockSpec(memory_space=pltpu.VMEM)
    return pl.pallas_call(
        functools.partial(total_kernel, nl, nr),
        out_shape=jax.ShapeDtypeStruct(x.shape, jnp.float32),
        in_specs=[vmem],
        out_specs=vmem,
        scratch_shapes=[
            pltpu.VMEM(x.shape, jnp.bfloat16),
            pltpu.VMEM((nl - 1, rows, 128), jnp.bfloat16),
            pltpu.VMEM((rows, 128), jnp.bfloat16),
            pltpu.VMEM((nr, rows, 128), jnp.bfloat16),
            pltpu.VMEM(x.shape, jnp.bfloat16),
            dma((nl - 1,)), dma((nl - 1,)),
            dma((nr - 1,)), dma((nr - 1,)),
            dma((nl - 1,)), dma((nl - 1,)),
        ],
        compiler_params=pltpu.CompilerParams(collective_id=0, has_side_effects=True),
    )(x)


def summed_everywhere(parts):
    nl, nr = lax.axis_size("lon"), lax.axis_size("rep")
    flat = jnp.concatenate([p.reshape(-1) for p in parts])
    unit = nl * 16 * 128
    size = -(-flat.shape[0] // unit) * unit
    flat = jnp.pad(flat, (0, size - flat.shape[0])).reshape(-1, 128)
    flat = total_over_all(flat, nl, nr).reshape(-1)
    out, at = [], 0
    for p in parts:
        out.append(flat[at : at + p.size].reshape(p.shape))
        at += p.size
    return out


def extended_2(cells, sides, width):
    for axis, dim in sides:
        count = lax.axis_size(axis)
        head = lax.slice_in_dim(cells, 0, width, axis=dim)
        tail = lax.slice_in_dim(cells, cells.shape[dim] - width, cells.shape[dim], axis=dim)
        cells = jnp.concatenate(
            [
                lax.ppermute(tail, axis, [(i, (i + 1) % count) for i in range(count)]),
                cells,
                lax.ppermute(head, axis, [((i + 1) % count, i) for i in range(count)]),
            ],
            axis=dim,
        )
    return cells


def shifted(value, axis, steps):
    count = lax.axis_size(axis)
    pairs = [(source, (source + steps) % count) for source in range(count)]
    return lax.ppermute(value, axis, pairs)


def conv_forward(padded, weight, stride):
    return lax.conv_general_dilated(
        padded,
        weight,
        (stride, stride),
        "VALID",
        dimension_numbers=("NCHW", "OIHW", "NCHW"),
        preferred_element_type=jnp.float32,
    )


def conv_weight_grad(padded, cotangent, kernel, stride):
    out_rows, out_cols = (cotangent.shape[2], cotangent.shape[3])
    reach_rows = stride * (out_rows - 1) + kernel
    reach_cols = stride * (out_cols - 1) + kernel
    used = padded[:, :, :reach_rows, :reach_cols]
    return lax.conv_general_dilated(
        used,
        cotangent,
        (1, 1),
        "VALID",
        rhs_dilation=(stride, stride),
        dimension_numbers=("CNHW", "IOHW", "CNHW"),
        preferred_element_type=jnp.float32,
    )


def conv_input_grad(cotangent, weight, stride, padded_shape):
    kernel = weight.shape[2]
    out_rows, out_cols = (cotangent.shape[2], cotangent.shape[3])
    high_rows = padded_shape[2] - (stride * (out_rows - 1) + 1)
    high_cols = padded_shape[3] - (stride * (out_cols - 1) + 1)
    flipped = weight[:, :, ::-1, ::-1]
    return lax.conv_general_dilated(
        cotangent,
        flipped,
        (1, 1),
        ((kernel - 1, high_rows), (kernel - 1, high_cols)),
        lhs_dilation=(stride, stride),
        dimension_numbers=("NCHW", "IOHW", "NCHW"),
        preferred_element_type=jnp.float32,
    )


def slope(values):
    sigma = jax.nn.sigmoid(values)
    return sigma * (1.0 + values * (1.0 - sigma))


def lat_pad(field, before, after):
    return jnp.pad(field, ((0, 0), (0, 0), (0, 0), (before, after)))


def head_pass(mid_act, head_weight, out_weight, pred_cotangent):
    head_padded = lat_pad(
        jnp.concatenate([mid_act[:, :, -1:], mid_act, mid_act[:, :, :1]], 2), 1, 1
    )
    head_pre = conv_forward(head_padded, head_weight, 1)
    head_act = jax.nn.silu(head_pre).astype(jnp.bfloat16)
    head_wide = head_act.astype(jnp.float32)
    prediction = jnp.einsum("c,schw->shw", out_weight, head_wide)
    head_cot = (pred_cotangent[:, None] * out_weight[None, :, None, None] * slope(head_pre)).astype(
        jnp.bfloat16
    )
    out_sum = jnp.einsum("shw,schw->c", pred_cotangent, head_wide)
    head_sum = conv_weight_grad(head_padded, head_cot, 3, 1)
    head_spread = conv_input_grad(head_cot, head_weight, 1, head_padded.shape)
    mid_grad = head_spread[:, :, 1:-1, 1:-1]
    mid_grad = (
        mid_grad.at[:, :, -1]
        .add(head_spread[:, :, 0, 1:-1])
        .at[:, :, 0]
        .add(head_spread[:, :, -1, 1:-1])
    )
    return (prediction, mid_grad.astype(jnp.bfloat16), head_sum, out_sum)


def head_totals(head_sum, out_sum):
    return (head_sum, out_sum)


def local(fields, stem_weight, mid_weight, head_weight, out_weight, pred_cotangent):
    extended = extended_2(fields, (("lon", 2),), 1)
    padded_fields = lat_pad(extended, 1, 1)
    stem_pre = conv_forward(padded_fields, stem_weight, 2)
    stem_act = jax.nn.silu(stem_pre).astype(jnp.bfloat16)
    left_side = shifted(stem_act[:, :, -1:], "lon", 1)
    mid_padded = lat_pad(jnp.concatenate([left_side, stem_act], 2), 1, 0)
    mid_pre = conv_forward(mid_padded, mid_weight, 2)
    mid_act = jax.nn.silu(mid_pre).astype(jnp.bfloat16)
    mid_whole = lax.all_to_all(mid_act, "lon", split_axis=0, concat_axis=2, tiled=True)
    prediction, mid_whole_grad, head_sum, out_sum = head_pass(
        mid_whole, head_weight, out_weight, pred_cotangent
    )
    head_sum, out_sum = head_totals(head_sum, out_sum)
    mid_grad = lax.all_to_all(mid_whole_grad, "lon", split_axis=2, concat_axis=0, tiled=True)
    mid_cot = (mid_grad.astype(jnp.float32) * slope(mid_pre)).astype(jnp.bfloat16)
    mid_sum = conv_weight_grad(mid_padded, mid_cot, 3, 2)
    mid_spread = conv_input_grad(mid_cot, mid_weight, 2, mid_padded.shape)
    edge_part = shifted(mid_spread[:, :, 0:1, 1:].astype(jnp.bfloat16), "lon", -1).astype(
        jnp.float32
    )
    stem_grad = mid_spread[:, :, 1:, 1:].at[:, :, -1:].add(edge_part).astype(jnp.bfloat16)
    stem_cotangent = (stem_grad.astype(jnp.float32) * slope(stem_pre)).astype(jnp.bfloat16)
    stem_sum = conv_weight_grad(padded_fields, stem_cotangent, 4, 2)
    stem_sum, mid_sum, head_sum, out_sum = summed_everywhere(
        (stem_sum, mid_sum, head_sum, out_sum)
    )
    factor = 1.0 / (fields.shape[0] * lax.axis_size("rep"))
    return (
        prediction,
        stem_cotangent,
        stem_sum * factor,
        mid_sum * factor,
        head_sum * factor,
        out_sum * factor,
    )


def solution(mesh):
    placed = (P("rep", None, "lon", None), P(), P(), P(), P(), P(("rep", "lon"), None, None))
    return jax.shard_map(
        local,
        mesh=mesh,
        in_specs=placed,
        out_specs=(P(("rep", "lon"), None, None), P("rep", None, "lon", None), P(), P(), P(), P()),
        check_vma=False,
    )
```

```python
import functools

import jax
import jax.numpy as jnp
from jax import lax
from jax.experimental import pallas as pl
from jax.experimental.pallas import tpu as pltpu
from jax.sharding import PartitionSpec as P

MESH = pl.DeviceIdType.MESH
F32 = jnp.float32
BF16 = jnp.bfloat16
C_IN, C_WIDE, C1, C2 = 24, 32, 32, 64


def grid_of(rows, cols):
    return (
        lax.broadcasted_iota(jnp.int32, (rows, cols), 0),
        lax.broadcasted_iota(jnp.int32, (rows, cols), 1),
    )


def ones_where(hit):
    return jnp.where(hit, 1.0, 0.0).astype(BF16)


def stem_pick():
    r, c = grid_of(256, 512)
    return ones_where(r == 2 * (c & 127) + (c >> 7) - 1)


def slab_order(width):
    r, c = grid_of(width * C_WIDE, C_IN * width)
    channel = r & (C_WIDE - 1)
    return ones_where((c == channel * width + (r >> 5)) & (channel < C_IN))


def mid_pick():
    r, c = grid_of(256, 384)
    return ones_where(((r >> 7) == ((c >> 6) & 1)) & ((r & 127) == 2 * (c & 63) + (c >> 7) - 1))


def mid_spread():
    r, c = grid_of(128, 768)
    return ones_where(
        ((r >> 6) == ((c >> 7) & 1)) & ((c & 127) == 2 * (r & 63) + (c >> 8) - 1)
    )


def dot(a, b, dims=((1,), (0,))):
    return lax.dot_general(a, b, (dims, ((), ())), preferred_element_type=F32)


def sigmoid(v):
    return 1.0 / (1.0 + jnp.exp(-v))


def slope_of(v, g):
    return g * (1.0 + v * (1.0 - g))


def swapped(tile):
    return pltpu.roll(tile, 64, axis=1)


def lon_shift(x, step):
    if step == 0:
        return x
    if step == 1:
        return jnp.concatenate([x[:, 128:], swapped(x[:, :128])], axis=1)
    return jnp.concatenate([swapped(x[:, -128:]), x[:, :-128]], axis=1)


def lat_shift(x, step):
    if step == 0:
        return x
    n = x.shape[1]
    lat = lax.broadcasted_iota(jnp.int32, x.shape, 1) & 63
    if step == 1:
        return jnp.where(lat == 63, 0.0, pltpu.roll(x, n - 1, axis=1))
    return jnp.where(lat == 0, 0.0, pltpu.roll(x, 1, axis=1))


def kernel(
    nl, nr, scen,
    fields, ws, wm, wmb, wh, ow, pc,
    pred, cot_out, g_stem, g_mid, g_head, g_out,
    got, e_buf, a_rows, f_buf, v_buf, m_rows, col_r, cc, cot_send,
    x_buf, half, got1, mine, got2, got3,
    own_sem, sf, rf, sc, rc, s1, r1, s2, r2, s3, r3,
):
    me, rep = lax.axis_index("lon"), lax.axis_index("rep")
    width = fields.shape[1] // C_IN
    per = width // 2
    lonh = nl * per
    hl = lonh // 2
    tiles = hl // 2

    def lon_peer(k):
        return (lax.rem(me + k, nl), rep)

    def rep_peer(k):
        return (me, lax.rem(rep + k, nr))

    def remote(src, dst, send, recv, peer):
        copy = pltpu.make_async_remote_copy(
            src_ref=src, dst_ref=dst, send_sem=send, recv_sem=recv,
            device_id=peer, device_id_type=MESH,
        )
        copy.start()
        return copy

    own = pltpu.make_async_copy(fields.at[me], got.at[me], own_sem.at[0])
    own.start()
    barrier = pltpu.get_barrier_semaphore()
    for k in range(1, nl):
        pl.semaphore_signal(barrier, inc=1, device_id=lon_peer(k), device_id_type=MESH)
    for k in range(1, nr):
        pl.semaphore_signal(barrier, inc=1, device_id=rep_peer(k), device_id_type=MESH)
    pl.semaphore_wait(barrier, nl - 1 + nr - 1)
    sends = []
    moved = []
    for k in range(1, nl):
        to = lax.rem(me + k, nl)
        moved.append(
            remote(fields.at[to], got.at[me], sf.at[k - 1], rf.at[k - 1], lon_peer(k))
        )
    sends += moved

    pick = stem_pick()
    order = slab_order(width)
    for k in range(nl):
        if k == 0:
            own.wait()
            source = me
        else:
            moved[k - 1].wait_recv()
            source = lax.rem(me - k + nl, nl)
        lines = dot(order, got[source]).astype(BF16)
        taps = dot(lines, pick).astype(BF16)
        for l in range(width):
            at = (l % 2 == 0)
            tile = source * per + l // 2 + (0 if at else 1)
            where = pl.ds(pl.multiple_of(tile * 128, 128), 128)
            for b in range(4):
                row = (128 if at else 0) + b * C_WIDE
                e_buf[row : row + C_WIDE, where] = taps[
                    l * C_WIDE : (l + 1) * C_WIDE, b * 128 : (b + 1) * 128
                ]
    e_buf[0:128, 0:128] = e_buf[0:128, lonh * 128 :]
    e_buf[128:256, lonh * 128 :] = e_buf[128:256, 0:128]

    both = dot(ws[...], e_buf[...])
    stem_pre = both[:C1, : lonh * 128] + both[C1:, 128:]
    stem_g = sigmoid(stem_pre)
    stem_act = (stem_pre * stem_g).astype(BF16)
    stem_slope = slope_of(stem_pre, stem_g)

    for l in range(hl):
        a_rows[l * C1 : (l + 1) * C1, 0:128] = stem_act[:, l * 128 : (l + 1) * 128]
        a_rows[l * C1 : (l + 1) * C1, 128:256] = stem_act[:, (l + hl) * 128 : (l + hl + 1) * 128]
    u = dot(a_rows[...], mid_pick())
    ub = u.astype(BF16)
    for b in range(3):
        last = u[(hl - 1) * C1 : hl * C1, b * 128 : (b + 1) * 128]
        f_buf[b * C1 : (b + 1) * C1, 0:128] = swapped(last).astype(BF16)
        for l in range(hl):
            t = (l + 1) // 2
            row = (96 if l % 2 == 0 else 0) + b * C1
            f_buf[row : row + C1, t * 128 : (t + 1) * 128] = ub[
                l * C1 : (l + 1) * C1, b * 128 : (b + 1) * 128
            ]
    n = tiles * 128
    mid_pre = dot(wm[0:192, :], f_buf[:, 0:n], ((0,), (0,))) + dot(
        wm[192:288, :], f_buf[0:96, 128 : n + 128], ((0,), (0,))
    )
    mid_g = sigmoid(mid_pre)
    mid_act = (mid_pre * mid_g).astype(BF16)
    mid_slope = slope_of(mid_pre, mid_g)

    y = dot(wh[...], mid_act)
    head_pre = None
    for b in range(3):
        s = None
        for a in range(3):
            block = (a * 3 + b) * C2
            part = lon_shift(y[block : block + C2], a - 1)
            s = part if s is None else s + part
        s = lat_shift(s, b - 1)
        head_pre = s if head_pre is None else head_pre + s
    head_g = sigmoid(head_pre)
    head_act = (head_pre * head_g).astype(BF16).astype(F32)
    pred[...] = jnp.sum(head_act * ow[...], axis=0, keepdims=True)
    out_sum = jnp.sum(head_act * pc[...], axis=1, keepdims=True)
    head_cot = (pc[...] * ow[...] * slope_of(head_pre, head_g)).astype(BF16).astype(F32)
    for b in range(3):
        moved_lat = lat_shift(head_cot, 1 - b)
        for a in range(3):
            block = (a * 3 + b) * C2
            col_r[block : block + C2, :] = lon_shift(moved_lat, 1 - a).astype(BF16)
    head_sum = dot(col_r[...], mid_act, ((1,), (1,)))
    mid_grad = dot(wh[...], col_r[...], ((0,), (0,))).astype(BF16).astype(F32)
    mid_cot = (mid_grad * mid_slope).astype(BF16)

    mid_sum_01 = dot(f_buf[:, 0:n], mid_cot, ((1,), (1,)))
    mid_sum_2 = dot(f_buf[0:96, 128 : n + 128], mid_cot, ((1,), (1,)))
    for t in range(tiles):
        m_rows[t * C2 : (t + 1) * C2, :] = mid_cot[:, t * 128 : (t + 1) * 128]
    up = dot(m_rows[...], mid_spread()).astype(BF16)
    for t in range(tiles):
        for b in range(3):
            for q in range(2):
                lon = t + q * tiles
                v_buf[b * C2 : (b + 1) * C2, lon * 128 : (lon + 1) * 128] = up[
                    t * C2 : (t + 1) * C2, b * 256 + q * 128 : b * 256 + (q + 1) * 128
                ]
    d = dot(wmb[...], v_buf[...])
    cc[0:C1, lonh * 128 :] = jnp.zeros((C1, 128), BF16)
    cc[C1 : 2 * C1, 0:128] = jnp.zeros((C1, 128), BF16)
    for i in range(lonh):
        m = i // 2
        if i % 2 == 0:
            grad = d[C1 : 2 * C1, m * 128 : (m + 1) * 128]
        else:
            nxt = (m + 1) % (lonh // 2)
            grad = d[2 * C1 :, m * 128 : (m + 1) * 128] + d[:C1, nxt * 128 : (nxt + 1) * 128]
        cot = grad.astype(BF16).astype(F32) * stem_slope[:, i * 128 : (i + 1) * 128]
        cot = cot.astype(BF16)
        cc[0:C1, i * 128 : (i + 1) * 128] = cot
        cc[C1 : 2 * C1, (i + 1) * 128 : (i + 2) * 128] = cot
        cot_send[i // per, :, (i % per) * 128 : (i % per + 1) * 128] = cot
    back = []
    for k in range(1, nl):
        to = lax.rem(me + k, nl)
        back.append(
            remote(cot_send.at[to], cot_out.at[me], sc.at[k - 1], rc.at[k - 1], lon_peer(k))
        )
    sends += back
    own_back = pltpu.make_async_copy(cot_send.at[me], cot_out.at[me], own_sem.at[1])
    own_back.start()
    stem_sum = dot(e_buf[...], cc[...], ((1,), (1,)))

    total_rows = x_buf.shape[0]
    rows = total_rows // nl
    left = [head_sum, jnp.broadcast_to(out_sum, (C2, C2))]
    right = [mid_sum_01, mid_sum_2, stem_sum]
    if total_rows > 640:
        left.append(jnp.zeros((total_rows - 640, 64), F32))
    right.append(jnp.zeros((total_rows - 544, 64), F32))
    x = jnp.concatenate(
        [jnp.concatenate(left, axis=0), jnp.concatenate(right, axis=0)], axis=1
    )
    x_buf[...] = x
    half[...] = x.astype(BF16)

    def part_of(at):
        return pl.ds(pl.multiple_of(at * rows, 16), rows)

    first = []
    for k in range(1, nl):
        to = lax.rem(me + k, nl)
        first.append(
            remote(half.at[part_of(to)], got1.at[k - 1], s1.at[k - 1], r1.at[k - 1], lon_peer(k))
        )
    total = x_buf[part_of(me), :]
    for k in range(1, nl):
        first[k - 1].wait_recv()
        total = total + got1[k - 1].astype(F32)
    mine[...] = total.astype(BF16)
    second = []
    for k in range(1, nr):
        second.append(remote(mine, got2.at[rep], s2.at[k - 1], r2.at[k - 1], rep_peer(k)))
    got2[rep] = mine[...]
    for copy in second:
        copy.wait_recv()
    total = got2[0].astype(F32)
    for k in range(1, nr):
        total = total + got2[k].astype(F32)
    got3[part_of(me), :] = total.astype(BF16)
    third = []
    for k in range(1, nl):
        third.append(
            remote(
                got3.at[part_of(me)], got3.at[part_of(me)], s3.at[k - 1], r3.at[k - 1], lon_peer(k)
            )
        )
    for copy in third:
        copy.wait_recv()
    factor = 1.0 / scen
    summed = got3[...].astype(F32) * factor
    g_head[...] = summed[0:576, 0:64]
    g_out[...] = summed[576:640, 0:1]
    g_mid[...] = summed[0:288, 64:128]
    g_stem[...] = summed[288:544, 64:128]
    own_back.wait()
    for copy in back:
        copy.wait_recv()
    for copy in sends + first + second + third:
        copy.wait_send()


def local(nl, nr, fields, stem_weight, mid_weight, head_weight, out_weight, pred_cotangent):
    scen_here, _, width, lat = fields.shape
    per = width // 2
    lonh = nl * per
    tiles = lonh // 4
    lonc = 2 * tiles
    x_rows = -(-640 // (nl * 16)) * nl * 16
    rows = x_rows // nl
    ws = jnp.pad(stem_weight, ((0, 0), (0, C_WIDE - C_IN), (0, 0), (0, 0)))
    ws = ws.reshape(C1, C_WIDE, 2, 2, 4).transpose(2, 0, 3, 4, 1).reshape(2 * C1, 256)
    wm = mid_weight.transpose(2, 3, 1, 0).reshape(288, C2)
    wmb = mid_weight.transpose(2, 1, 3, 0).reshape(96, 192)
    wh = head_weight.transpose(2, 3, 0, 1).reshape(576, C2)
    pc = pred_cotangent.reshape(2, tiles, 64).transpose(1, 0, 2).reshape(1, tiles * 128)
    vmem = pl.BlockSpec(memory_space=pltpu.VMEM)
    hbm = pl.BlockSpec(memory_space=pl.ANY)
    dma = pltpu.SemaphoreType.DMA
    pred, cot, g_stem, g_mid, g_head, g_out = pl.pallas_call(
        functools.partial(kernel, nl, nr, scen_here * nr),
        out_shape=[
            jax.ShapeDtypeStruct((1, tiles * 128), F32),
            jax.ShapeDtypeStruct((nl, C1, per * 128), BF16),
            jax.ShapeDtypeStruct((256, C2), F32),
            jax.ShapeDtypeStruct((288, C2), F32),
            jax.ShapeDtypeStruct((576, C2), F32),
            jax.ShapeDtypeStruct((C2, 1), F32),
        ],
        in_specs=[hbm] + [vmem] * 6,
        out_specs=[vmem, hbm, vmem, vmem, vmem, vmem],
        scratch_shapes=[
            pltpu.VMEM((nl, C_IN * width, lat), BF16),
            pltpu.VMEM((256, (lonh + 1) * 128), BF16),
            pltpu.VMEM((lonh // 2 * C1, 256), BF16),
            pltpu.VMEM((192, (tiles + 1) * 128), BF16),
            pltpu.VMEM((192, lonc * 128), BF16),
            pltpu.VMEM((tiles * C2, 128), BF16),
            pltpu.VMEM((576, tiles * 128), BF16),
            pltpu.VMEM((2 * C1, (lonh + 1) * 128), BF16),
            pltpu.VMEM((nl, C1, per * 128), BF16),
            pltpu.VMEM((x_rows, 128), F32),
            pltpu.VMEM((x_rows, 128), BF16),
            pltpu.VMEM((nl - 1, rows, 128), BF16),
            pltpu.VMEM((rows, 128), BF16),
            pltpu.VMEM((nr, rows, 128), BF16),
            pltpu.VMEM((x_rows, 128), BF16),
            dma((2,)),
            dma((nl - 1,)), dma((nl - 1,)),
            dma((nl - 1,)), dma((nl - 1,)),
            dma((nl - 1,)), dma((nl - 1,)),
            dma((nr - 1,)), dma((nr - 1,)),
            dma((nl - 1,)), dma((nl - 1,)),
        ],
        compiler_params=pltpu.CompilerParams(
            collective_id=0, has_side_effects=True, vmem_limit_bytes=50 * 2**20
        ),
    )(
        fields.reshape(scen_here, C_IN * width, lat),
        ws, wm, wmb, wh, out_weight.reshape(C2, 1), pc,
    )
    prediction = pred.reshape(tiles, 2, 64).transpose(1, 0, 2).reshape(1, lonc, 64)
    stem_cotangent = cot.reshape(nl, C1, per, 128)
    grad_stem = g_stem.reshape(2, 4, C_WIDE, 2, C1)[:, :, :C_IN].transpose(4, 2, 3, 0, 1)
    grad_stem = grad_stem.reshape(C1, C_IN, 4, 4)
    grad_mid = g_mid.reshape(3, 3, C1, C2).transpose(3, 2, 0, 1)
    grad_head = g_head.reshape(3, 3, C2, C2).transpose(2, 3, 0, 1)
    return prediction, stem_cotangent, grad_stem, grad_mid, grad_head, g_out.reshape(C2)


def solution(mesh):
    placed = (P("rep", None, "lon", None), P(), P(), P(), P(), P(("rep", "lon"), None, None))
    return jax.shard_map(
        functools.partial(local, mesh.shape["lon"], mesh.shape["rep"]),
        mesh=mesh,
        in_specs=placed,
        out_specs=(P(("rep", "lon"), None, None), P("rep", None, "lon", None), P(), P(), P(), P()),
        check_vma=False,
    )
```

```python
import functools

import jax
import jax.numpy as jnp
from jax import lax
from jax.experimental import pallas as pl
from jax.experimental.pallas import tpu as pltpu
from jax.sharding import PartitionSpec as P

MESH = pl.DeviceIdType.MESH
F32 = jnp.float32
BF16 = jnp.bfloat16
C_IN, C_WIDE, C1, C2 = 24, 32, 32, 64


def grid_of(rows, cols):
    return (
        lax.broadcasted_iota(jnp.int32, (rows, cols), 0),
        lax.broadcasted_iota(jnp.int32, (rows, cols), 1),
    )


def ones_where(hit):
    return jnp.where(hit, 1.0, 0.0).astype(BF16)


def stem_pick():
    r, c = grid_of(256, 512)
    return ones_where(r == 2 * (c & 127) + (c >> 7) - 1)


def slab_order(width):
    r, c = grid_of(width * C_WIDE, C_IN * width)
    channel = r & (C_WIDE - 1)
    return ones_where((c == channel * width + (r >> 5)) & (channel < C_IN))


def mid_pick():
    r, c = grid_of(256, 384)
    return ones_where(((r >> 7) == ((c >> 6) & 1)) & ((r & 127) == 2 * (c & 63) + (c >> 7) - 1))


def mid_spread():
    r, c = grid_of(128, 768)
    return ones_where(
        ((r >> 6) == ((c >> 7) & 1)) & ((c & 127) == 2 * (r & 63) + (c >> 8) - 1)
    )


def stem_order(ah):
    r, c = grid_of(C_IN * 16, 256)
    return ones_where(r == (c & 31) * 16 + (2 * ah + (c >> 7)) * 4 + ((c >> 5) & 3))


def stem_rows():
    r, c = grid_of(C_IN * 16, 128)
    return ones_where(c == (r & 3) * C_WIDE + (r >> 4))


def dot(a, b, dims=((1,), (0,))):
    return lax.dot_general(a, b, (dims, ((), ())), preferred_element_type=F32)


def sigmoid(v):
    return 1.0 / (1.0 + jnp.exp(-v))


def slope_of(v, g):
    return g * (1.0 + v * (1.0 - g))


def swapped(tile):
    return pltpu.roll(tile, 64, axis=1)


def lon_shift(x, step):
    if step == 0:
        return x
    if step == 1:
        return jnp.concatenate([x[:, 128:], swapped(x[:, :128])], axis=1)
    return jnp.concatenate([swapped(x[:, -128:]), x[:, :-128]], axis=1)


def lat_shift(x, step):
    if step == 0:
        return x
    n = x.shape[1]
    lat = lax.broadcasted_iota(jnp.int32, x.shape, 1) & 63
    if step == 1:
        return jnp.where(lat == 63, 0.0, pltpu.roll(x, n - 1, axis=1))
    return jnp.where(lat == 0, 0.0, pltpu.roll(x, 1, axis=1))


def kernel(
    nl, nr,
    fields, ws_hbm, wm_hbm, wh_hbm, ow_in, pc_in,
    pred, cot_out, all_a, all_b,
    ws, wm, wh,
    got, e_buf, a_rows, f_buf, v_buf, m_rows, col_r, cc, cot_send,
    sum_a, half_a, one_a, mine_a, two_a,
    sum_b, half_b, one_b, mine_b, two_b,
    own_sem, w_sem, sf, rf, sc, rc,
    s1a, r1a, s2a, r2a, s3a, r3a,
    s1b, r1b, s2b, r2b, s3b, r3b,
):
    me, rep = lax.axis_index("lon"), lax.axis_index("rep")
    width = fields.shape[1] // C_IN
    per = width // 2
    lonh = nl * per
    hl = lonh // 2
    tiles = hl // 2

    def lon_peer(k):
        return (lax.rem(me + k, nl), rep)

    def rep_peer(k):
        return (me, lax.rem(rep + k, nr))

    def remote(src, dst, send, recv, peer):
        copy = pltpu.make_async_remote_copy(
            src_ref=src, dst_ref=dst, send_sem=send, recv_sem=recv,
            device_id=peer, device_id_type=MESH,
        )
        copy.start()
        return copy

    own = pltpu.make_async_copy(fields.at[me], got.at[me], own_sem.at[0])
    own.start()
    loads = []
    for i, (src, dst) in enumerate(((ws_hbm, ws), (wm_hbm, wm), (wh_hbm, wh))):
        load = pltpu.make_async_copy(src, dst, w_sem.at[i])
        load.start()
        loads.append(load)
    barrier = pltpu.get_barrier_semaphore()
    for k in range(1, nl):
        pl.semaphore_signal(barrier, inc=1, device_id=lon_peer(k), device_id_type=MESH)
    for k in range(1, nr):
        pl.semaphore_signal(barrier, inc=1, device_id=rep_peer(k), device_id_type=MESH)
    pl.semaphore_wait(barrier, nl - 1 + nr - 1)
    sends = []
    moved = []
    for k in range(1, nl):
        to = lax.rem(me + k, nl)
        moved.append(
            remote(fields.at[to], got.at[me], sf.at[k - 1], rf.at[k - 1], lon_peer(k))
        )
    sends += moved

    def spread_out(x, y, sums, halves, one, send, recv):
        x = jnp.concatenate([x, y], axis=1)
        pad = sums.shape[0] - x.shape[0]
        if pad:
            x = jnp.concatenate([x, jnp.zeros((pad, 128), F32)], axis=0)
        sums[...] = x
        halves[...] = x.astype(BF16)
        rows = sums.shape[0] // nl
        copies = []
        for k in range(1, nl):
            to = pl.ds(pl.multiple_of(lax.rem(me + k, nl) * rows, 16), rows)
            copies.append(
                remote(halves.at[to], one.at[k - 1], send.at[k - 1], recv.at[k - 1], lon_peer(k))
            )
        return copies

    def across(copies, sums, one, mine, two, send, recv):
        rows = sums.shape[0] // nl
        total = sums[pl.ds(pl.multiple_of(me * rows, 16), rows), :]
        for k in range(1, nl):
            copies[k - 1].wait_recv()
            total = total + one[k - 1].astype(F32)
        mine[...] = total.astype(BF16)
        out = []
        for k in range(1, nr):
            out.append(remote(mine, two.at[rep], send.at[k - 1], recv.at[k - 1], rep_peer(k)))
        two[rep] = mine[...]
        return out

    def gather(copies, two, everywhere, send, recv):
        rows = everywhere.shape[0] // nl
        for copy in copies:
            copy.wait_recv()
        total = two[0].astype(F32)
        for k in range(1, nr):
            total = total + two[k].astype(F32)
        here = pl.ds(pl.multiple_of(me * rows, 16), rows)
        everywhere[here, :] = total.astype(BF16)
        out = []
        for k in range(1, nl):
            out.append(
                remote(
                    everywhere.at[here], everywhere.at[here],
                    send.at[k - 1], recv.at[k - 1], lon_peer(k),
                )
            )
        return out

    pick = stem_pick()
    order = slab_order(width)
    for k in range(nl):
        if k == 0:
            own.wait()
            source = me
        else:
            moved[k - 1].wait_recv()
            source = lax.rem(me - k + nl, nl)
        lines = dot(order, got[source]).astype(BF16)
        taps = dot(lines, pick).astype(BF16)
        for l in range(width):
            at = (l % 2 == 0)
            tile = source * per + l // 2 + (0 if at else 1)
            where = pl.ds(pl.multiple_of(tile * 128, 128), 128)
            for b in range(4):
                row = (128 if at else 0) + b * C_WIDE
                e_buf[row : row + C_WIDE, where] = taps[
                    l * C_WIDE : (l + 1) * C_WIDE, b * 128 : (b + 1) * 128
                ]
    e_buf[0:128, 0:128] = e_buf[0:128, lonh * 128 :]
    e_buf[128:256, lonh * 128 :] = e_buf[128:256, 0:128]

    for load in loads:
        load.wait()
    ws_rows = ws[...].astype(F32).reshape(C_IN * 16, C1).astype(BF16)
    ws_all = jnp.concatenate(
        [dot(ws_rows, stem_order(ah), ((0,), (0,))) for ah in range(2)], axis=0
    ).astype(BF16)
    both = dot(ws_all, e_buf[...])
    stem_pre = both[:C1, : lonh * 128] + both[C1:, 128:]
    stem_g = sigmoid(stem_pre)
    stem_act = (stem_pre * stem_g).astype(BF16)
    stem_slope = slope_of(stem_pre, stem_g)

    for l in range(hl):
        a_rows[l * C1 : (l + 1) * C1, 0:128] = stem_act[:, l * 128 : (l + 1) * 128]
        a_rows[l * C1 : (l + 1) * C1, 128:256] = stem_act[:, (l + hl) * 128 : (l + hl + 1) * 128]
    u = dot(a_rows[...], mid_pick())
    ub = u.astype(BF16)
    for b in range(3):
        last = u[(hl - 1) * C1 : hl * C1, b * 128 : (b + 1) * 128]
        f_buf[b * C1 : (b + 1) * C1, 0:128] = swapped(last).astype(BF16)
        for l in range(hl):
            t = (l + 1) // 2
            row = (96 if l % 2 == 0 else 0) + b * C1
            f_buf[row : row + C1, t * 128 : (t + 1) * 128] = ub[
                l * C1 : (l + 1) * C1, b * 128 : (b + 1) * 128
            ]
    n = tiles * 128
    mid_pre = dot(wm[0:192, :], f_buf[:, 0:n], ((0,), (0,))) + dot(
        wm[192:288, :], f_buf[0:96, 128 : n + 128], ((0,), (0,))
    )
    mid_g = sigmoid(mid_pre)
    mid_act = (mid_pre * mid_g).astype(BF16)
    mid_slope = slope_of(mid_pre, mid_g)

    y = dot(wh[...], mid_act)
    head_pre = None
    for b in range(3):
        s = None
        for a in range(3):
            block = (a * 3 + b) * C2
            part = lon_shift(y[block : block + C2], a - 1)
            s = part if s is None else s + part
        s = lat_shift(s, b - 1)
        head_pre = s if head_pre is None else head_pre + s
    head_g = sigmoid(head_pre)
    head_act = (head_pre * head_g).astype(BF16).astype(F32)
    r, c = grid_of(C2, C2)
    ow = jnp.sum(jnp.where(r == c, ow_in[...], 0.0), axis=1, keepdims=True)
    pc = jnp.concatenate([pc_in[0:tiles, :], pc_in[tiles:, :]], axis=1)
    pc = jnp.concatenate([pc[t : t + 1, :] for t in range(tiles)], axis=1)
    pred[...] = jnp.sum(head_act * ow, axis=0, keepdims=True)
    out_sum = jnp.sum(head_act * pc, axis=1, keepdims=True)
    head_cot = (pc * ow * slope_of(head_pre, head_g)).astype(BF16).astype(F32)
    for b in range(3):
        moved_lat = lat_shift(head_cot, 1 - b)
        for a in range(3):
            block = (a * 3 + b) * C2
            col_r[block : block + C2, :] = lon_shift(moved_lat, 1 - a).astype(BF16)
    head_sum = dot(col_r[...], mid_act, ((1,), (1,)))
    mid_grad = dot(wh[...], col_r[...], ((0,), (0,))).astype(BF16).astype(F32)
    mid_cot = (mid_grad * mid_slope).astype(BF16)

    mid_sum_01 = dot(f_buf[:, 0:n], mid_cot, ((1,), (1,)))
    mid_sum_2 = dot(f_buf[0:96, 128 : n + 128], mid_cot, ((1,), (1,)))
    block_a = jnp.concatenate(
        [head_sum, jnp.broadcast_to(out_sum, (C2, C2)), mid_sum_01, mid_sum_2], axis=0
    )
    first_a = spread_out(block_a[:464], block_a[464:], sum_a, half_a, one_a, s1a, r1a)
    for t in range(tiles):
        m_rows[t * C2 : (t + 1) * C2, :] = mid_cot[:, t * 128 : (t + 1) * 128]
    up = dot(m_rows[...], mid_spread()).astype(BF16)
    for t in range(tiles):
        for b in range(3):
            for q in range(2):
                lon = t + q * tiles
                v_buf[b * C2 : (b + 1) * C2, lon * 128 : (lon + 1) * 128] = up[
                    t * C2 : (t + 1) * C2, b * 256 + q * 128 : b * 256 + (q + 1) * 128
                ]
    wide = wm[...].astype(F32)
    wmb = jnp.concatenate(
        [
            jnp.concatenate(
                [wide[(a * 3 + b) * C1 : (a * 3 + b + 1) * C1] for a in range(3)], axis=0
            )
            for b in range(3)
        ],
        axis=1,
    ).astype(BF16)
    d = dot(wmb, v_buf[...])
    cc[0:C1, lonh * 128 :] = jnp.zeros((C1, 128), BF16)
    cc[C1 : 2 * C1, 0:128] = jnp.zeros((C1, 128), BF16)
    for i in range(lonh):
        m = i // 2
        if i % 2 == 0:
            grad = d[C1 : 2 * C1, m * 128 : (m + 1) * 128]
        else:
            nxt = (m + 1) % (lonh // 2)
            grad = d[2 * C1 :, m * 128 : (m + 1) * 128] + d[:C1, nxt * 128 : (nxt + 1) * 128]
        cot = grad.astype(BF16).astype(F32) * stem_slope[:, i * 128 : (i + 1) * 128]
        cot = cot.astype(BF16)
        cc[0:C1, i * 128 : (i + 1) * 128] = cot
        cc[C1 : 2 * C1, (i + 1) * 128 : (i + 2) * 128] = cot
        cot_send[i // per, :, (i % per) * 128 : (i % per + 1) * 128] = cot
    second_a = across(first_a, sum_a, one_a, mine_a, two_a, s2a, r2a)
    stem_sum = dot(e_buf[...], cc[...], ((1,), (1,)))
    first_b = spread_out(stem_sum[:128], stem_sum[128:], sum_b, half_b, one_b, s1b, r1b)
    third_a = gather(second_a, two_a, all_a, s3a, r3a)
    back = []
    for k in range(1, nl):
        to = lax.rem(me + k, nl)
        back.append(
            remote(cot_send.at[to], cot_out.at[me], sc.at[k - 1], rc.at[k - 1], lon_peer(k))
        )
    own_back = pltpu.make_async_copy(cot_send.at[me], cot_out.at[me], own_sem.at[1])
    own_back.start()
    second_b = across(first_b, sum_b, one_b, mine_b, two_b, s2b, r2b)
    third_b = gather(second_b, two_b, all_b, s3b, r3b)
    for copy in third_a + back + third_b:
        copy.wait_recv()
    own_back.wait()
    for copy in moved + first_a + second_a + third_a + back + first_b + second_b + third_b:
        copy.wait_send()


def finish(factor, pred, cot, all_a, all_b, pred_out, cot_out, g_stem, g_mid, g_head, g_out):
    tiles = pred.shape[1] // 128
    lines = jnp.concatenate(
        [pred[:, t * 128 : (t + 1) * 128] for t in range(tiles)], axis=0
    )
    pred_out[0:tiles, :] = lines[:, 0:64]
    pred_out[tiles:, :] = lines[:, 64:128]
    a = all_a[0:464, :].astype(F32) * factor
    g_head[0:464, :] = a[:, 0:64]
    g_head[464:576, :] = a[0:112, 64:128]
    r, c = grid_of(C2, C2)
    g_out[...] = jnp.sum(
        jnp.where(r == c, a[112:176, 64:128], 0.0), axis=0, keepdims=True
    )
    g_mid[...] = a[176:464, 64:128]
    rows = dot(stem_rows(), all_b[0:128, :])
    r, c = grid_of(C_IN * 16, 128)
    group = (r >> 2) & 3
    kept = jnp.where((c >> 5) == (group & 1) * 2 + (group >> 1), rows, 0.0).astype(BF16)
    r, c = grid_of(128, C1)
    stem = dot(kept, ones_where((r & 31) == c)) * factor
    g_stem[...] = stem.reshape(g_stem.shape)
    for s in range(cot.shape[0]):
        whole = cot[s].astype(F32)
        cot_out[s] = whole.reshape(cot_out.shape[1:]).astype(BF16)


def local(nl, nr, fields, stem_weight, mid_weight, head_weight, out_weight, pred_cotangent):
    scen_here, _, width, lat = fields.shape
    per = width // 2
    lonh = nl * per
    tiles = lonh // 4
    lonc = 2 * tiles
    ws = stem_weight.transpose(1, 2, 3, 0).reshape(C_IN * 4, 4, C1)
    wm = mid_weight.transpose(2, 3, 1, 0).reshape(288, C2)
    wh = head_weight.transpose(2, 3, 0, 1).reshape(576, C2)
    vmem = pl.BlockSpec(memory_space=pltpu.VMEM)
    hbm = pl.BlockSpec(memory_space=pltpu.HBM)
    dma = pltpu.SemaphoreType.DMA

    def sum_scratch(size):
        return [
            pltpu.VMEM((size, 128), F32),
            pltpu.VMEM((size, 128), BF16),
            pltpu.VMEM((nl - 1, size // nl, 128), BF16),
            pltpu.VMEM((size // nl, 128), BF16),
            pltpu.VMEM((nr, size // nl, 128), BF16),
        ]

    sum_sems = [
        dma((nl - 1,)), dma((nl - 1,)),
        dma((nr - 1,)), dma((nr - 1,)),
        dma((nl - 1,)), dma((nl - 1,)),
    ]
    size_a = -(-464 // (nl * 16)) * nl * 16
    size_b = -(-128 // (nl * 16)) * nl * 16
    pred, cot, all_a, all_b = pl.pallas_call(
        functools.partial(kernel, nl, nr),
        out_shape=[
            jax.ShapeDtypeStruct((1, tiles * 128), F32),
            jax.ShapeDtypeStruct((nl, C1, per * 128), BF16),
            jax.ShapeDtypeStruct((size_a, 128), BF16),
            jax.ShapeDtypeStruct((size_b, 128), BF16),
        ],
        in_specs=[hbm] * 4 + [vmem] * 2,
        out_specs=[vmem] * 4,
        scratch_shapes=[
            pltpu.VMEM(ws.shape, BF16),
            pltpu.VMEM(wm.shape, BF16),
            pltpu.VMEM(wh.shape, BF16),
            pltpu.VMEM((nl, C_IN * width, lat), BF16),
            pltpu.VMEM((256, (lonh + 1) * 128), BF16),
            pltpu.VMEM((lonh // 2 * C1, 256), BF16),
            pltpu.VMEM((192, (tiles + 1) * 128), BF16),
            pltpu.VMEM((192, lonc * 128), BF16),
            pltpu.VMEM((tiles * C2, 128), BF16),
            pltpu.VMEM((576, tiles * 128), BF16),
            pltpu.VMEM((2 * C1, (lonh + 1) * 128), BF16),
            pltpu.VMEM((nl, C1, per * 128), BF16),
        ]
        + sum_scratch(size_a)
        + sum_scratch(size_b)
        + [
            dma((2,)), dma((3,)),
            dma((nl - 1,)), dma((nl - 1,)),
            dma((nl - 1,)), dma((nl - 1,)),
        ]
        + sum_sems
        + sum_sems,
        compiler_params=pltpu.CompilerParams(
            collective_id=0, has_side_effects=True, vmem_limit_bytes=48 * 2**20
        ),
    )(
        fields.reshape(scen_here, C_IN * width, lat),
        ws, wm, wh, out_weight.reshape(1, C2), pred_cotangent.reshape(lonc, 64),
    )
    prediction, stem_cotangent, g_stem, g_mid, g_head, g_out = pl.pallas_call(
        functools.partial(finish, 1.0 / (scen_here * nr)),
        out_shape=[
            jax.ShapeDtypeStruct((lonc, 64), F32),
            jax.ShapeDtypeStruct((nl, C1, per, 128), BF16),
            jax.ShapeDtypeStruct((C_IN * 4, 4, C1), F32),
            jax.ShapeDtypeStruct((288, C2), F32),
            jax.ShapeDtypeStruct((576, C2), F32),
            jax.ShapeDtypeStruct((1, C2), F32),
        ],
        in_specs=[vmem] * 4,
        out_specs=[vmem] * 6,
        compiler_params=pltpu.CompilerParams(vmem_limit_bytes=32 * 2**20),
    )(pred, cot, all_a, all_b)
    grad_stem = g_stem.reshape(C_IN, 4, 4, C1).transpose(3, 0, 1, 2)
    grad_mid = g_mid.reshape(3, 3, C1, C2).transpose(3, 2, 0, 1)
    grad_head = g_head.reshape(3, 3, C2, C2).transpose(2, 3, 0, 1)
    return (
        prediction.reshape(1, lonc, 64), stem_cotangent,
        grad_stem, grad_mid, grad_head, g_out.reshape(C2),
    )


def solution(mesh):
    placed = (P("rep", None, "lon", None), P(), P(), P(), P(), P(("rep", "lon"), None, None))
    return jax.shard_map(
        functools.partial(local, mesh.shape["lon"], mesh.shape["rep"]),
        mesh=mesh,
        in_specs=placed,
        out_specs=(P(("rep", "lon"), None, None), P("rep", None, "lon", None), P(), P(), P(), P()),
        check_vma=False,
    )
```

```python
import functools

import jax
import jax.numpy as jnp
from jax import lax
from jax.experimental import pallas as pl
from jax.experimental.pallas import tpu as pltpu
from jax.sharding import PartitionSpec as P

MESH = pl.DeviceIdType.MESH
F32 = jnp.float32
BF16 = jnp.bfloat16
C_IN, C_WIDE, C1, C2 = 24, 32, 32, 64


def grid_of(rows, cols):
    return (
        lax.broadcasted_iota(jnp.int32, (rows, cols), 0),
        lax.broadcasted_iota(jnp.int32, (rows, cols), 1),
    )


def ones_where(hit):
    return jnp.where(hit, 1.0, 0.0).astype(BF16)


def stem_pick():
    r, c = grid_of(256, 512)
    return ones_where(r == 2 * (c & 127) + (c >> 7) - 1)


def slab_order(width):
    r, c = grid_of(width * C_WIDE, C_IN * width)
    channel = r & (C_WIDE - 1)
    return ones_where((c == channel * width + (r >> 5)) & (channel < C_IN))


def mid_pick():
    r, c = grid_of(256, 384)
    return ones_where(((r >> 7) == ((c >> 6) & 1)) & ((r & 127) == 2 * (c & 63) + (c >> 7) - 1))


def mid_spread():
    r, c = grid_of(128, 768)
    return ones_where(
        ((r >> 6) == ((c >> 7) & 1)) & ((c & 127) == 2 * (r & 63) + (c >> 8) - 1)
    )


def stem_order(ah):
    r, c = grid_of(C_IN * 16, 256)
    return ones_where(r == (c & 31) * 16 + (2 * ah + (c >> 7)) * 4 + ((c >> 5) & 3))


def stem_rows():
    r, c = grid_of(C_IN * 16, 128)
    return ones_where(c == (r & 3) * C_WIDE + (r >> 4))


def dot(a, b, dims=((1,), (0,))):
    return lax.dot_general(a, b, (dims, ((), ())), preferred_element_type=F32)


def sigmoid(v):
    return 1.0 / (1.0 + jnp.exp(-v))


def slope_of(v, g):
    return g * (1.0 + v * (1.0 - g))


def swapped(tile):
    return pltpu.roll(tile, 64, axis=1)


def lon_shift(x, step):
    if step == 0:
        return x
    if step == 1:
        return jnp.concatenate([x[:, 128:], swapped(x[:, :128])], axis=1)
    return jnp.concatenate([swapped(x[:, -128:]), x[:, :-128]], axis=1)


def lat_shift(x, step):
    if step == 0:
        return x
    n = x.shape[1]
    lat = lax.broadcasted_iota(jnp.int32, x.shape, 1) & 63
    if step == 1:
        return jnp.where(lat == 63, 0.0, pltpu.roll(x, n - 1, axis=1))
    return jnp.where(lat == 0, 0.0, pltpu.roll(x, 1, axis=1))


def kernel(
    nl, nr,
    fields, ws_hbm, wm_hbm, wh_hbm, ow_hbm, pc_hbm,
    pred, cot_out, all_a, all_b,
    ws, wm, wh, ow_in, pc_in,
    ws_all, wmb, pick_mid, spread_mid, y_buf,
    got, e_buf, a_rows, f_buf, v_buf, m_rows, col_r, cc, cot_send,
    sum_a, half_a, one_a, mine_a, two_a,
    sum_b, half_b, one_b, mine_b, two_b,
    own_sem, w_sem, sf, rf, sc, rc,
    s1a, r1a, s2a, r2a, s3a, r3a,
    s1b, r1b, s2b, r2b, s3b, r3b,
):
    me, rep = lax.axis_index("lon"), lax.axis_index("rep")
    width = fields.shape[1] // C_IN
    per = width // 2
    lonh = nl * per
    hl = lonh // 2
    tiles = hl // 2

    def lon_peer(k):
        return (lax.rem(me + k, nl), rep)

    def rep_peer(k):
        return (me, lax.rem(rep + k, nr))

    def remote(src, dst, send, recv, peer):
        copy = pltpu.make_async_remote_copy(
            src_ref=src, dst_ref=dst, send_sem=send, recv_sem=recv,
            device_id=peer, device_id_type=MESH,
        )
        copy.start()
        return copy

    own = pltpu.make_async_copy(fields.at[me], got.at[me], own_sem.at[0])
    own.start()
    loads = []
    for i, (src, dst) in enumerate(((ws_hbm, ws), (wm_hbm, wm), (wh_hbm, wh), (ow_hbm, ow_in), (pc_hbm, pc_in))):
        load = pltpu.make_async_copy(src, dst, w_sem.at[i])
        load.start()
        loads.append(load)
    barrier = pltpu.get_barrier_semaphore()
    for k in range(1, nl):
        pl.semaphore_signal(barrier, inc=1, device_id=lon_peer(k), device_id_type=MESH)
    for k in range(1, nr):
        pl.semaphore_signal(barrier, inc=1, device_id=rep_peer(k), device_id_type=MESH)
    pl.semaphore_wait(barrier, nl - 1 + nr - 1)
    sends = []
    moved = []
    for k in range(1, nl):
        to = lax.rem(me + k, nl)
        moved.append(
            remote(fields.at[to], got.at[me], sf.at[k - 1], rf.at[k - 1], lon_peer(k))
        )
    sends += moved

    def spread_out(x, y, sums, halves, one, send, recv):
        x = jnp.concatenate([x, y], axis=1)
        pad = sums.shape[0] - x.shape[0]
        if pad:
            x = jnp.concatenate([x, jnp.zeros((pad, 128), F32)], axis=0)
        sums[...] = x
        halves[...] = x.astype(BF16)
        rows = sums.shape[0] // nl
        copies = []
        for k in range(1, nl):
            to = pl.ds(pl.multiple_of(lax.rem(me + k, nl) * rows, 16), rows)
            copies.append(
                remote(halves.at[to], one.at[k - 1], send.at[k - 1], recv.at[k - 1], lon_peer(k))
            )
        return copies

    def across(copies, sums, one, mine, two, send, recv):
        rows = sums.shape[0] // nl
        total = sums[pl.ds(pl.multiple_of(me * rows, 16), rows), :]
        for k in range(1, nl):
            copies[k - 1].wait_recv()
            total = total + one[k - 1].astype(F32)
        mine[...] = total.astype(BF16)
        out = []
        for k in range(1, nr):
            out.append(remote(mine, two.at[rep], send.at[k - 1], recv.at[k - 1], rep_peer(k)))
        two[rep] = mine[...]
        return out

    def gather(copies, two, everywhere, send, recv):
        rows = everywhere.shape[0] // nl
        for copy in copies:
            copy.wait_recv()
        total = two[0].astype(F32)
        for k in range(1, nr):
            total = total + two[k].astype(F32)
        here = pl.ds(pl.multiple_of(me * rows, 16), rows)
        everywhere[here, :] = total.astype(BF16)
        out = []
        for k in range(1, nl):
            out.append(
                remote(
                    everywhere.at[here], everywhere.at[here],
                    send.at[k - 1], recv.at[k - 1], lon_peer(k),
                )
            )
        return out

    for load in loads:
        load.wait()
    ws_rows = ws[...].astype(F32).reshape(C_IN * 16, C1).astype(BF16)
    for ah in range(2):
        ws_all[ah * C1 : (ah + 1) * C1, :] = dot(
            ws_rows, stem_order(ah), ((0,), (0,))
        ).astype(BF16)
    wide = wm[...].astype(F32)
    wmb[...] = jnp.concatenate(
        [
            jnp.concatenate(
                [wide[(a * 3 + b) * C1 : (a * 3 + b + 1) * C1] for a in range(3)], axis=0
            )
            for b in range(3)
        ],
        axis=1,
    ).astype(BF16)
    pick_mid[...] = mid_pick()
    spread_mid[...] = mid_spread()
    pick = stem_pick()
    order = slab_order(width)
    group = per * 128

    def stem_group(g):
        where = pl.ds(pl.multiple_of(g * group, 128), group)
        y_buf[:, where] = dot(ws_all[...], e_buf[:, where])

    for k in range(nl):
        if k == 0:
            own.wait()
            source = me
        else:
            moved[k - 1].wait_recv()
            source = lax.rem(me - k + nl, nl)
        lines = dot(order, got[source]).astype(BF16)
        taps = dot(lines, pick).astype(BF16)
        for l in range(width):
            even = l % 2 == 0
            tile = source * per + l // 2 - (1 if even else 0)
            if l == 0:
                tile = lax.rem(tile + lonh, lonh)
            where = pl.ds(pl.multiple_of(tile * 128, 128), 128)
            for b in range(4):
                row = (128 if even else 0) + b * C_WIDE
                e_buf[row : row + C_WIDE, where] = taps[
                    l * C_WIDE : (l + 1) * C_WIDE, b * 128 : (b + 1) * 128
                ]
        if k > 0:
            stem_group(source)
    stem_group(me)

    last = (lonh - 1) * 128
    stem_pre = (
        jnp.concatenate([y_buf[0:C1, last:], y_buf[0:C1, :last]], axis=1) + y_buf[C1:, :]
    )
    stem_g = sigmoid(stem_pre)
    stem_act = (stem_pre * stem_g).astype(BF16)
    stem_slope = slope_of(stem_pre, stem_g)

    for l in range(hl):
        a_rows[l * C1 : (l + 1) * C1, 0:128] = stem_act[:, l * 128 : (l + 1) * 128]
        a_rows[l * C1 : (l + 1) * C1, 128:256] = stem_act[:, (l + hl) * 128 : (l + hl + 1) * 128]
    u = dot(a_rows[...], pick_mid[...])
    ub = u.astype(BF16)
    for b in range(3):
        last = u[(hl - 1) * C1 : hl * C1, b * 128 : (b + 1) * 128]
        f_buf[b * C1 : (b + 1) * C1, 0:128] = swapped(last).astype(BF16)
        for l in range(hl):
            t = (l + 1) // 2
            row = (96 if l % 2 == 0 else 0) + b * C1
            f_buf[row : row + C1, t * 128 : (t + 1) * 128] = ub[
                l * C1 : (l + 1) * C1, b * 128 : (b + 1) * 128
            ]
    n = tiles * 128
    mid_pre = dot(wm[0:192, :], f_buf[:, 0:n], ((0,), (0,))) + dot(
        wm[192:288, :], f_buf[0:96, 128 : n + 128], ((0,), (0,))
    )
    mid_g = sigmoid(mid_pre)
    mid_act = (mid_pre * mid_g).astype(BF16)
    mid_slope = slope_of(mid_pre, mid_g)

    y = dot(wh[...], mid_act)
    head_pre = None
    for b in range(3):
        s = None
        for a in range(3):
            block = (a * 3 + b) * C2
            part = lon_shift(y[block : block + C2], a - 1)
            s = part if s is None else s + part
        s = lat_shift(s, b - 1)
        head_pre = s if head_pre is None else head_pre + s
    head_g = sigmoid(head_pre)
    head_act = (head_pre * head_g).astype(BF16).astype(F32)
    r, c = grid_of(C2, C2)
    ow = jnp.sum(jnp.where(r == c, ow_in[...], 0.0), axis=1, keepdims=True)
    pc = jnp.concatenate([pc_in[0:tiles, :], pc_in[tiles:, :]], axis=1)
    pc = jnp.concatenate([pc[t : t + 1, :] for t in range(tiles)], axis=1)
    pred[...] = jnp.sum(head_act * ow, axis=0, keepdims=True)
    out_sum = jnp.sum(head_act * pc, axis=1, keepdims=True)
    head_cot = (pc * ow * slope_of(head_pre, head_g)).astype(BF16).astype(F32)
    for b in range(3):
        moved_lat = lat_shift(head_cot, 1 - b)
        for a in range(3):
            block = (a * 3 + b) * C2
            col_r[block : block + C2, :] = lon_shift(moved_lat, 1 - a).astype(BF16)
    head_sum = dot(col_r[...], mid_act, ((1,), (1,)))
    mid_grad = dot(wh[...], col_r[...], ((0,), (0,))).astype(BF16).astype(F32)
    mid_cot = (mid_grad * mid_slope).astype(BF16)

    mid_sum_01 = dot(f_buf[:, 0:n], mid_cot, ((1,), (1,)))
    mid_sum_2 = dot(f_buf[0:96, 128 : n + 128], mid_cot, ((1,), (1,)))
    block_a = jnp.concatenate(
        [head_sum, jnp.broadcast_to(out_sum, (C2, C2)), mid_sum_01, mid_sum_2], axis=0
    )
    first_a = spread_out(block_a[:464], block_a[464:], sum_a, half_a, one_a, s1a, r1a)
    for t in range(tiles):
        m_rows[t * C2 : (t + 1) * C2, :] = mid_cot[:, t * 128 : (t + 1) * 128]
    up = dot(m_rows[...], spread_mid[...]).astype(BF16)
    for t in range(tiles):
        for b in range(3):
            for q in range(2):
                lon = t + q * tiles
                v_buf[b * C2 : (b + 1) * C2, lon * 128 : (lon + 1) * 128] = up[
                    t * C2 : (t + 1) * C2, b * 256 + q * 128 : b * 256 + (q + 1) * 128
                ]
    d = dot(wmb[...], v_buf[...])
    for i in range(lonh):
        m = i // 2
        if i % 2 == 0:
            grad = d[C1 : 2 * C1, m * 128 : (m + 1) * 128]
        else:
            nxt = (m + 1) % (lonh // 2)
            grad = d[2 * C1 :, m * 128 : (m + 1) * 128] + d[:C1, nxt * 128 : (nxt + 1) * 128]
        cot = grad.astype(BF16).astype(F32) * stem_slope[:, i * 128 : (i + 1) * 128]
        cot = cot.astype(BF16)
        before = (i - 1) % lonh
        cc[0:C1, before * 128 : (before + 1) * 128] = cot
        cc[C1 : 2 * C1, i * 128 : (i + 1) * 128] = cot
        cot_send[i // per, :, (i % per) * 128 : (i % per + 1) * 128] = cot
    second_a = across(first_a, sum_a, one_a, mine_a, two_a, s2a, r2a)
    stem_sum = dot(e_buf[...], cc[...], ((1,), (1,)))
    first_b = spread_out(stem_sum[:128], stem_sum[128:], sum_b, half_b, one_b, s1b, r1b)
    third_a = gather(second_a, two_a, all_a, s3a, r3a)
    back = []
    for k in range(1, nl):
        to = lax.rem(me + k, nl)
        back.append(
            remote(cot_send.at[to], cot_out.at[me], sc.at[k - 1], rc.at[k - 1], lon_peer(k))
        )
    own_back = pltpu.make_async_copy(cot_send.at[me], cot_out.at[me], own_sem.at[1])
    own_back.start()
    for copy in moved + first_a:
        copy.wait_send()
    second_b = across(first_b, sum_b, one_b, mine_b, two_b, s2b, r2b)
    for copy in second_a + third_a:
        copy.wait_send()
    third_b = gather(second_b, two_b, all_b, s3b, r3b)
    own_back.wait()
    for copy in first_b + second_b:
        copy.wait_send()
    for copy in third_a + back + third_b:
        copy.wait_recv()
    for copy in back + third_b:
        copy.wait_send()


def finish(factor, pred, cot, all_a, all_b, pred_out, cot_out, g_stem, g_mid, g_head, g_out):
    tiles = pred.shape[1] // 128
    lines = jnp.concatenate(
        [pred[:, t * 128 : (t + 1) * 128] for t in range(tiles)], axis=0
    )
    pred_out[0:tiles, :] = lines[:, 0:64]
    pred_out[tiles:, :] = lines[:, 64:128]
    a = all_a[0:464, :].astype(F32) * factor
    g_head[0:464, :] = a[:, 0:64]
    g_head[464:576, :] = a[0:112, 64:128]
    r, c = grid_of(C2, C2)
    g_out[...] = jnp.sum(
        jnp.where(r == c, a[112:176, 64:128], 0.0), axis=0, keepdims=True
    )
    g_mid[...] = a[176:464, 64:128]
    rows = dot(stem_rows(), all_b[0:128, :])
    r, c = grid_of(C_IN * 16, 128)
    group = (r >> 2) & 3
    kept = jnp.where((c >> 5) == (group & 1) * 2 + (group >> 1), rows, 0.0).astype(BF16)
    r, c = grid_of(128, C1)
    stem = dot(kept, ones_where((r & 31) == c)) * factor
    g_stem[...] = stem.reshape(g_stem.shape)
    for s in range(cot.shape[0]):
        whole = cot[s].astype(F32)
        cot_out[s] = whole.reshape(cot_out.shape[1:]).astype(BF16)


def local(nl, nr, fields, stem_weight, mid_weight, head_weight, out_weight, pred_cotangent):
    scen_here, _, width, lat = fields.shape
    per = width // 2
    lonh = nl * per
    tiles = lonh // 4
    lonc = 2 * tiles
    ws = stem_weight.transpose(1, 2, 3, 0).reshape(C_IN * 4, 4, C1)
    wm = mid_weight.transpose(2, 3, 1, 0).reshape(288, C2)
    wh = head_weight.transpose(2, 3, 0, 1).reshape(576, C2)
    vmem = pl.BlockSpec(memory_space=pltpu.VMEM)
    hbm = pl.BlockSpec(memory_space=pltpu.HBM)
    dma = pltpu.SemaphoreType.DMA

    def sum_scratch(size):
        return [
            pltpu.VMEM((size, 128), F32),
            pltpu.VMEM((size, 128), BF16),
            pltpu.VMEM((nl - 1, size // nl, 128), BF16),
            pltpu.VMEM((size // nl, 128), BF16),
            pltpu.VMEM((nr, size // nl, 128), BF16),
        ]

    sum_sems = [
        dma((nl - 1,)), dma((nl - 1,)),
        dma((nr - 1,)), dma((nr - 1,)),
        dma((nl - 1,)), dma((nl - 1,)),
    ]
    size_a = -(-464 // (nl * 16)) * nl * 16
    size_b = -(-128 // (nl * 16)) * nl * 16
    pred, cot, all_a, all_b = pl.pallas_call(
        functools.partial(kernel, nl, nr),
        out_shape=[
            jax.ShapeDtypeStruct((1, tiles * 128), F32),
            jax.ShapeDtypeStruct((nl, C1, per * 128), BF16),
            jax.ShapeDtypeStruct((size_a, 128), BF16),
            jax.ShapeDtypeStruct((size_b, 128), BF16),
        ],
        in_specs=[hbm] * 6,
        out_specs=[vmem, hbm, vmem, vmem],
        scratch_shapes=[
            pltpu.VMEM(ws.shape, BF16),
            pltpu.VMEM(wm.shape, BF16),
            pltpu.VMEM(wh.shape, BF16),
            pltpu.VMEM((1, C2), F32),
            pltpu.VMEM((lonc, 64), F32),
            pltpu.VMEM((2 * C1, 256), BF16),
            pltpu.VMEM((96, 192), BF16),
            pltpu.VMEM((256, 384), BF16),
            pltpu.VMEM((128, 768), BF16),
            pltpu.VMEM((2 * C1, lonh * 128), F32),
            pltpu.VMEM((nl, C_IN * width, lat), BF16),
            pltpu.VMEM((256, lonh * 128), BF16),
            pltpu.VMEM((lonh // 2 * C1, 256), BF16),
            pltpu.VMEM((192, (tiles + 1) * 128), BF16),
            pltpu.VMEM((192, lonc * 128), BF16),
            pltpu.VMEM((tiles * C2, 128), BF16),
            pltpu.VMEM((576, tiles * 128), BF16),
            pltpu.VMEM((2 * C1, lonh * 128), BF16),
            pltpu.VMEM((nl, C1, per * 128), BF16),
        ]
        + sum_scratch(size_a)
        + sum_scratch(size_b)
        + [
            dma((2,)), dma((5,)),
            dma((nl - 1,)), dma((nl - 1,)),
            dma((nl - 1,)), dma((nl - 1,)),
        ]
        + sum_sems
        + sum_sems,
        compiler_params=pltpu.CompilerParams(
            collective_id=0, has_side_effects=True, vmem_limit_bytes=60 * 2**20
        ),
    )(
        fields.reshape(scen_here, C_IN * width, lat),
        ws, wm, wh, out_weight.reshape(1, C2), pred_cotangent.reshape(lonc, 64),
    )
    prediction, stem_cotangent, g_stem, g_mid, g_head, g_out = pl.pallas_call(
        functools.partial(finish, 1.0 / (scen_here * nr)),
        out_shape=[
            jax.ShapeDtypeStruct((lonc, 64), F32),
            jax.ShapeDtypeStruct((nl, C1, per, 128), BF16),
            jax.ShapeDtypeStruct((C_IN * 4, 4, C1), F32),
            jax.ShapeDtypeStruct((288, C2), F32),
            jax.ShapeDtypeStruct((576, C2), F32),
            jax.ShapeDtypeStruct((1, C2), F32),
        ],
        in_specs=[vmem] * 4,
        out_specs=[vmem] * 6,
        compiler_params=pltpu.CompilerParams(vmem_limit_bytes=60 * 2**20),
    )(pred, cot, all_a, all_b)
    grad_stem = g_stem.reshape(C_IN, 4, 4, C1).transpose(3, 0, 1, 2)
    grad_mid = g_mid.reshape(3, 3, C1, C2).transpose(3, 2, 0, 1)
    grad_head = g_head.reshape(3, 3, C2, C2).transpose(2, 3, 0, 1)
    return (
        prediction.reshape(1, lonc, 64), stem_cotangent,
        grad_stem, grad_mid, grad_head, g_out.reshape(C2),
    )


def solution(mesh):
    placed = (P("rep", None, "lon", None), P(), P(), P(), P(), P(("rep", "lon"), None, None))
    return jax.shard_map(
        functools.partial(local, mesh.shape["lon"], mesh.shape["rep"]),
        mesh=mesh,
        in_specs=placed,
        out_specs=(P(("rep", "lon"), None, None), P("rep", None, "lon", None), P(), P(), P(), P()),
        check_vma=False,
    )
```

```python
import functools

import jax
import jax.numpy as jnp
from jax import lax
from jax.experimental import pallas as pl
from jax.experimental.pallas import tpu as pltpu
from jax.sharding import PartitionSpec as P

MESH = pl.DeviceIdType.MESH
F32 = jnp.float32
BF16 = jnp.bfloat16
C_IN, C_WIDE, C1, C2 = 24, 32, 32, 64


def grid_of(rows, cols):
    return (
        lax.broadcasted_iota(jnp.int32, (rows, cols), 0),
        lax.broadcasted_iota(jnp.int32, (rows, cols), 1),
    )


def ones_where(hit):
    return jnp.where(hit, 1.0, 0.0).astype(BF16)


def stem_pick():
    r, c = grid_of(256, 512)
    return ones_where(r == 2 * (c & 127) + (c >> 7) - 1)


def slab_order(width):
    r, c = grid_of(width * C_WIDE, C_IN * width)
    channel = r & (C_WIDE - 1)
    return ones_where((c == channel * width + (r >> 5)) & (channel < C_IN))


def mid_pick():
    r, c = grid_of(256, 384)
    return ones_where(((r >> 7) == ((c >> 6) & 1)) & ((r & 127) == 2 * (c & 63) + (c >> 7) - 1))


def mid_spread():
    r, c = grid_of(128, 768)
    return ones_where(
        ((r >> 6) == ((c >> 7) & 1)) & ((c & 127) == 2 * (r & 63) + (c >> 8) - 1)
    )


def stem_order(ah):
    r, c = grid_of(C_IN * 16, 256)
    return ones_where(r == (c & 31) * 16 + (2 * ah + (c >> 7)) * 4 + ((c >> 5) & 3))


def stem_rows():
    r, c = grid_of(C_IN * 16, 128)
    return ones_where(c == (r & 3) * C_WIDE + (r >> 4))


def dot(a, b, dims=((1,), (0,))):
    return lax.dot_general(a, b, (dims, ((), ())), preferred_element_type=F32)


def sigmoid(v):
    return 0.5 + 0.5 * jnp.tanh(0.5 * v)


def slope_of(v, g):
    return g * (1.0 + v * (1.0 - g))


def swapped(tile):
    return pltpu.roll(tile, 64, axis=1)


def lon_shift(x, step):
    if step == 0:
        return x
    if step == 1:
        return jnp.concatenate([x[:, 128:], swapped(x[:, :128])], axis=1)
    return jnp.concatenate([swapped(x[:, -128:]), x[:, :-128]], axis=1)


def lat_shift(x, step):
    if step == 0:
        return x
    n = x.shape[1]
    lat = lax.broadcasted_iota(jnp.int32, x.shape, 1) & 63
    if step == 1:
        return jnp.where(lat == 63, 0.0, pltpu.roll(x, n - 1, axis=1))
    return jnp.where(lat == 0, 0.0, pltpu.roll(x, 1, axis=1))


def kernel(
    nl, nr,
    fields, ws_hbm, wm_hbm, wh_hbm, ow_hbm, pc_hbm,
    pred, cot_out, all_a, all_b,
    ws, wm, wh, ow_in, pc_in,
    ws_all, wmb, pick_mid, spread_mid, y_buf, slopes,
    got, e_buf, a_rows, f_buf, v_buf, m_rows, col_r, cc, cot_send,
    sum_a, half_a, one_a, mine_a, two_a,
    sum_b, half_b, one_b, mine_b, two_b,
    own_sem, w_sem, sf, rf, sc, rc,
    s1a, r1a, s2a, r2a, s3a, r3a,
    s1b, r1b, s2b, r2b, s3b, r3b,
):
    me, rep = lax.axis_index("lon"), lax.axis_index("rep")
    width = fields.shape[1] // C_IN
    per = width // 2
    lonh = nl * per
    hl = lonh // 2
    tiles = hl // 2

    def lon_peer(k):
        return (lax.rem(me + k, nl), rep)

    def rep_peer(k):
        return (me, lax.rem(rep + k, nr))

    def remote(src, dst, send, recv, peer):
        copy = pltpu.make_async_remote_copy(
            src_ref=src, dst_ref=dst, send_sem=send, recv_sem=recv,
            device_id=peer, device_id_type=MESH,
        )
        copy.start()
        return copy

    own = pltpu.make_async_copy(fields.at[me], got.at[me], own_sem.at[0])
    own.start()
    loads = []
    for i, (src, dst) in enumerate(((ws_hbm, ws), (wm_hbm, wm), (wh_hbm, wh), (ow_hbm, ow_in), (pc_hbm, pc_in))):
        load = pltpu.make_async_copy(src, dst, w_sem.at[i])
        load.start()
        loads.append(load)
    barrier = pltpu.get_barrier_semaphore()
    for k in range(1, nl):
        pl.semaphore_signal(barrier, inc=1, device_id=lon_peer(k), device_id_type=MESH)
    for k in range(1, nr):
        pl.semaphore_signal(barrier, inc=1, device_id=rep_peer(k), device_id_type=MESH)
    pl.semaphore_wait(barrier, nl - 1 + nr - 1)
    sends = []
    moved = []
    for k in range(1, nl):
        to = lax.rem(me + k, nl)
        moved.append(
            remote(fields.at[to], got.at[me], sf.at[k - 1], rf.at[k - 1], lon_peer(k))
        )
    sends += moved

    def spread_out(x, y, sums, halves, one, send, recv):
        x = jnp.concatenate([x, y], axis=1)
        pad = sums.shape[0] - x.shape[0]
        if pad:
            x = jnp.concatenate([x, jnp.zeros((pad, 128), F32)], axis=0)
        sums[...] = x
        halves[...] = x.astype(BF16)
        rows = sums.shape[0] // nl
        copies = []
        for k in range(1, nl):
            to = pl.ds(pl.multiple_of(lax.rem(me + k, nl) * rows, 16), rows)
            copies.append(
                remote(halves.at[to], one.at[k - 1], send.at[k - 1], recv.at[k - 1], lon_peer(k))
            )
        return copies

    def across(copies, sums, one, mine, two, send, recv):
        rows = sums.shape[0] // nl
        total = sums[pl.ds(pl.multiple_of(me * rows, 16), rows), :]
        for k in range(1, nl):
            copies[k - 1].wait_recv()
            total = total + one[k - 1].astype(F32)
        mine[...] = total.astype(BF16)
        out = []
        for k in range(1, nr):
            out.append(remote(mine, two.at[rep], send.at[k - 1], recv.at[k - 1], rep_peer(k)))
        two[rep] = mine[...]
        return out

    def gather(copies, two, everywhere, send, recv):
        rows = everywhere.shape[0] // nl
        for copy in copies:
            copy.wait_recv()
        total = two[0].astype(F32)
        for k in range(1, nr):
            total = total + two[k].astype(F32)
        here = pl.ds(pl.multiple_of(me * rows, 16), rows)
        everywhere[here, :] = total.astype(BF16)
        out = []
        for k in range(1, nl):
            out.append(
                remote(
                    everywhere.at[here], everywhere.at[here],
                    send.at[k - 1], recv.at[k - 1], lon_peer(k),
                )
            )
        return out

    for load in loads:
        load.wait()
    ws_rows = ws[...].astype(F32).reshape(C_IN * 16, C1).astype(BF16)
    for ah in range(2):
        ws_all[ah * C1 : (ah + 1) * C1, :] = dot(
            ws_rows, stem_order(ah), ((0,), (0,))
        ).astype(BF16)
    wide = wm[...].astype(F32)
    wmb[...] = jnp.concatenate(
        [
            jnp.concatenate(
                [wide[(a * 3 + b) * C1 : (a * 3 + b + 1) * C1] for a in range(3)], axis=0
            )
            for b in range(3)
        ],
        axis=1,
    ).astype(BF16)
    pick_mid[...] = mid_pick()
    spread_mid[...] = mid_spread()
    pick = stem_pick()
    order = slab_order(width)
    group = per * 128

    def stem_group(g):
        where = pl.ds(pl.multiple_of(g * group, 128), group)
        y_buf[:, where] = dot(ws_all[...], e_buf[:, where])

    def act_group(g):
        for i in range(per):
            tile = g * per + i
            here = pl.ds(pl.multiple_of(tile * 128, 128), 128)
            prior = lax.rem(tile - 1 + lonh, lonh) if i == 0 else tile - 1
            prior = pl.ds(pl.multiple_of(prior * 128, 128), 128)
            pre = y_buf[0:C1, prior] + y_buf[C1:, here]
            gate = sigmoid(pre)
            slopes[:, here] = slope_of(pre, gate)
            line = pl.ds(pl.multiple_of(lax.rem(tile, hl) * C1, C1), C1)
            half = pl.ds(pl.multiple_of(lax.div(tile, hl) * 128, 128), 128)
            a_rows[line, half] = (pre * gate).astype(BF16)

    for k in range(nl):
        if k == 0:
            own.wait()
            source = me
        else:
            moved[k - 1].wait_recv()
            source = lax.rem(me - k + nl, nl)
        lines = dot(order, got[source]).astype(BF16)
        taps = dot(lines, pick).astype(BF16)
        for l in range(width):
            even = l % 2 == 0
            tile = source * per + l // 2 - (1 if even else 0)
            if l == 0:
                tile = lax.rem(tile + lonh, lonh)
            where = pl.ds(pl.multiple_of(tile * 128, 128), 128)
            for b in range(4):
                row = (128 if even else 0) + b * C_WIDE
                e_buf[row : row + C_WIDE, where] = taps[
                    l * C_WIDE : (l + 1) * C_WIDE, b * 128 : (b + 1) * 128
                ]
        if k > 0:
            stem_group(source)
        if k > 1:
            act_group(lax.rem(source + 1, nl))
    stem_group(me)
    act_group(lax.rem(me + 1, nl))
    act_group(me)

    u = dot(a_rows[...], pick_mid[...])
    ub = u.astype(BF16)
    for b in range(3):
        last = u[(hl - 1) * C1 : hl * C1, b * 128 : (b + 1) * 128]
        f_buf[b * C1 : (b + 1) * C1, 0:128] = swapped(last).astype(BF16)
        for l in range(hl):
            t = (l + 1) // 2
            row = (96 if l % 2 == 0 else 0) + b * C1
            f_buf[row : row + C1, t * 128 : (t + 1) * 128] = ub[
                l * C1 : (l + 1) * C1, b * 128 : (b + 1) * 128
            ]
    n = tiles * 128
    mid_pre = dot(wm[0:192, :], f_buf[:, 0:n], ((0,), (0,))) + dot(
        wm[192:288, :], f_buf[0:96, 128 : n + 128], ((0,), (0,))
    )
    mid_g = sigmoid(mid_pre)
    mid_act = (mid_pre * mid_g).astype(BF16)
    mid_slope = slope_of(mid_pre, mid_g)

    y = dot(wh[...], mid_act)
    head_pre = None
    for b in range(3):
        s = None
        for a in range(3):
            block = (a * 3 + b) * C2
            part = lon_shift(y[block : block + C2], a - 1)
            s = part if s is None else s + part
        s = lat_shift(s, b - 1)
        head_pre = s if head_pre is None else head_pre + s
    head_g = sigmoid(head_pre)
    head_act = (head_pre * head_g).astype(BF16).astype(F32)
    r, c = grid_of(C2, C2)
    ow = jnp.sum(jnp.where(r == c, ow_in[...], 0.0), axis=1, keepdims=True)
    pc = jnp.concatenate([pc_in[0:tiles, :], pc_in[tiles:, :]], axis=1)
    pc = jnp.concatenate([pc[t : t + 1, :] for t in range(tiles)], axis=1)
    pred[...] = jnp.sum(head_act * ow, axis=0, keepdims=True)
    out_sum = jnp.sum(head_act * pc, axis=1, keepdims=True)
    head_cot = (pc * ow * slope_of(head_pre, head_g)).astype(BF16).astype(F32)
    for b in range(3):
        moved_lat = lat_shift(head_cot, 1 - b)
        for a in range(3):
            block = (a * 3 + b) * C2
            col_r[block : block + C2, :] = lon_shift(moved_lat, 1 - a).astype(BF16)
    head_sum = dot(col_r[...], mid_act, ((1,), (1,)))
    mid_grad = dot(wh[...], col_r[...], ((0,), (0,))).astype(BF16).astype(F32)
    mid_cot = (mid_grad * mid_slope).astype(BF16)

    mid_sum_01 = dot(f_buf[:, 0:n], mid_cot, ((1,), (1,)))
    mid_sum_2 = dot(f_buf[0:96, 128 : n + 128], mid_cot, ((1,), (1,)))
    block_a = jnp.concatenate(
        [head_sum, jnp.broadcast_to(out_sum, (C2, C2)), mid_sum_01, mid_sum_2], axis=0
    )
    first_a = spread_out(block_a[:464], block_a[464:], sum_a, half_a, one_a, s1a, r1a)
    for t in range(tiles):
        m_rows[t * C2 : (t + 1) * C2, :] = mid_cot[:, t * 128 : (t + 1) * 128]
    up = dot(m_rows[...], spread_mid[...]).astype(BF16)
    for t in range(tiles):
        for b in range(3):
            for q in range(2):
                lon = t + q * tiles
                v_buf[b * C2 : (b + 1) * C2, lon * 128 : (lon + 1) * 128] = up[
                    t * C2 : (t + 1) * C2, b * 256 + q * 128 : b * 256 + (q + 1) * 128
                ]
    d = dot(wmb[...], v_buf[...])
    second_a = across(first_a, sum_a, one_a, mine_a, two_a, s2a, r2a)
    for i in range(lonh):
        m = i // 2
        if i % 2 == 0:
            grad = d[C1 : 2 * C1, m * 128 : (m + 1) * 128]
        else:
            nxt = (m + 1) % (lonh // 2)
            grad = d[2 * C1 :, m * 128 : (m + 1) * 128] + d[:C1, nxt * 128 : (nxt + 1) * 128]
        cot = grad.astype(BF16).astype(F32) * slopes[:, i * 128 : (i + 1) * 128]
        cot = cot.astype(BF16)
        before = (i - 1) % lonh
        cc[0:C1, before * 128 : (before + 1) * 128] = cot
        cc[C1 : 2 * C1, i * 128 : (i + 1) * 128] = cot
        cot_send[i // per, :, (i % per) * 128 : (i % per + 1) * 128] = cot
    back = []
    for k in range(1, nl):
        to = lax.rem(me + k, nl)
        back.append(
            remote(cot_send.at[to], cot_out.at[me], sc.at[k - 1], rc.at[k - 1], lon_peer(k))
        )
    own_back = pltpu.make_async_copy(cot_send.at[me], cot_out.at[me], own_sem.at[1])
    own_back.start()
    stem_sum = dot(e_buf[...], cc[...], ((1,), (1,)))
    first_b = spread_out(stem_sum[:128], stem_sum[128:], sum_b, half_b, one_b, s1b, r1b)
    third_a = gather(second_a, two_a, all_a, s3a, r3a)
    for copy in moved + first_a:
        copy.wait_send()
    second_b = across(first_b, sum_b, one_b, mine_b, two_b, s2b, r2b)
    for copy in second_a + third_a:
        copy.wait_send()
    third_b = gather(second_b, two_b, all_b, s3b, r3b)
    own_back.wait()
    for copy in first_b + second_b:
        copy.wait_send()
    for copy in third_a + back + third_b:
        copy.wait_recv()
    for copy in back + third_b:
        copy.wait_send()


def finish(factor, pred, cot, all_a, all_b, pred_out, cot_out, g_stem, g_mid, g_head, g_out):
    tiles = pred.shape[1] // 128
    lines = jnp.concatenate(
        [pred[:, t * 128 : (t + 1) * 128] for t in range(tiles)], axis=0
    )
    pred_out[0:tiles, :] = lines[:, 0:64]
    pred_out[tiles:, :] = lines[:, 64:128]
    a = all_a[0:464, :].astype(F32) * factor
    g_head[0:464, :] = a[:, 0:64]
    g_head[464:576, :] = a[0:112, 64:128]
    r, c = grid_of(C2, C2)
    g_out[...] = jnp.sum(
        jnp.where(r == c, a[112:176, 64:128], 0.0), axis=0, keepdims=True
    )
    g_mid[...] = a[176:464, 64:128]
    rows = dot(stem_rows(), all_b[0:128, :])
    r, c = grid_of(C_IN * 16, 128)
    group = (r >> 2) & 3
    kept = jnp.where((c >> 5) == (group & 1) * 2 + (group >> 1), rows, 0.0).astype(BF16)
    r, c = grid_of(128, C1)
    stem = dot(kept, ones_where((r & 31) == c)) * factor
    g_stem[...] = stem.reshape(g_stem.shape)
    for s in range(cot.shape[0]):
        whole = cot[s].astype(F32)
        cot_out[s] = whole.reshape(cot_out.shape[1:]).astype(BF16)


def local(nl, nr, fields, stem_weight, mid_weight, head_weight, out_weight, pred_cotangent):
    scen_here, _, width, lat = fields.shape
    per = width // 2
    lonh = nl * per
    tiles = lonh // 4
    lonc = 2 * tiles
    ws = stem_weight.transpose(1, 2, 3, 0).reshape(C_IN * 4, 4, C1)
    wm = mid_weight.transpose(2, 3, 1, 0).reshape(288, C2)
    wh = head_weight.transpose(2, 3, 0, 1).reshape(576, C2)
    vmem = pl.BlockSpec(memory_space=pltpu.VMEM)
    hbm = pl.BlockSpec(memory_space=pltpu.HBM)
    dma = pltpu.SemaphoreType.DMA

    def sum_scratch(size):
        return [
            pltpu.VMEM((size, 128), F32),
            pltpu.VMEM((size, 128), BF16),
            pltpu.VMEM((nl - 1, size // nl, 128), BF16),
            pltpu.VMEM((size // nl, 128), BF16),
            pltpu.VMEM((nr, size // nl, 128), BF16),
        ]

    sum_sems = [
        dma((nl - 1,)), dma((nl - 1,)),
        dma((nr - 1,)), dma((nr - 1,)),
        dma((nl - 1,)), dma((nl - 1,)),
    ]
    size_a = -(-464 // (nl * 16)) * nl * 16
    size_b = -(-128 // (nl * 16)) * nl * 16
    pred, cot, all_a, all_b = pl.pallas_call(
        functools.partial(kernel, nl, nr),
        out_shape=[
            jax.ShapeDtypeStruct((1, tiles * 128), F32),
            jax.ShapeDtypeStruct((nl, C1, per * 128), BF16),
            jax.ShapeDtypeStruct((size_a, 128), BF16),
            jax.ShapeDtypeStruct((size_b, 128), BF16),
        ],
        in_specs=[hbm] * 6,
        out_specs=[vmem, hbm, vmem, vmem],
        scratch_shapes=[
            pltpu.VMEM(ws.shape, BF16),
            pltpu.VMEM(wm.shape, BF16),
            pltpu.VMEM(wh.shape, BF16),
            pltpu.VMEM((1, C2), F32),
            pltpu.VMEM((lonc, 64), F32),
            pltpu.VMEM((2 * C1, 256), BF16),
            pltpu.VMEM((96, 192), BF16),
            pltpu.VMEM((256, 384), BF16),
            pltpu.VMEM((128, 768), BF16),
            pltpu.VMEM((2 * C1, lonh * 128), F32),
            pltpu.VMEM((C1, lonh * 128), F32),
            pltpu.VMEM((nl, C_IN * width, lat), BF16),
            pltpu.VMEM((256, lonh * 128), BF16),
            pltpu.VMEM((lonh // 2 * C1, 256), BF16),
            pltpu.VMEM((192, (tiles + 1) * 128), BF16),
            pltpu.VMEM((192, lonc * 128), BF16),
            pltpu.VMEM((tiles * C2, 128), BF16),
            pltpu.VMEM((576, tiles * 128), BF16),
            pltpu.VMEM((2 * C1, lonh * 128), BF16),
            pltpu.VMEM((nl, C1, per * 128), BF16),
        ]
        + sum_scratch(size_a)
        + sum_scratch(size_b)
        + [
            dma((2,)), dma((5,)),
            dma((nl - 1,)), dma((nl - 1,)),
            dma((nl - 1,)), dma((nl - 1,)),
        ]
        + sum_sems
        + sum_sems,
        compiler_params=pltpu.CompilerParams(
            collective_id=0, has_side_effects=True, vmem_limit_bytes=60 * 2**20
        ),
    )(
        fields.reshape(scen_here, C_IN * width, lat),
        ws, wm, wh, out_weight.reshape(1, C2), pred_cotangent.reshape(lonc, 64),
    )
    prediction, stem_cotangent, g_stem, g_mid, g_head, g_out = pl.pallas_call(
        functools.partial(finish, 1.0 / (scen_here * nr)),
        out_shape=[
            jax.ShapeDtypeStruct((lonc, 64), F32),
            jax.ShapeDtypeStruct((nl, C1, per, 128), BF16),
            jax.ShapeDtypeStruct((C_IN * 4, 4, C1), F32),
            jax.ShapeDtypeStruct((288, C2), F32),
            jax.ShapeDtypeStruct((576, C2), F32),
            jax.ShapeDtypeStruct((1, C2), F32),
        ],
        in_specs=[vmem] * 4,
        out_specs=[vmem] * 6,
        compiler_params=pltpu.CompilerParams(vmem_limit_bytes=60 * 2**20),
    )(pred, cot, all_a, all_b)
    grad_stem = g_stem.reshape(C_IN, 4, 4, C1).transpose(3, 0, 1, 2)
    grad_mid = g_mid.reshape(3, 3, C1, C2).transpose(3, 2, 0, 1)
    grad_head = g_head.reshape(3, 3, C2, C2).transpose(2, 3, 0, 1)
    return (
        prediction.reshape(1, lonc, 64), stem_cotangent,
        grad_stem, grad_mid, grad_head, g_out.reshape(C2),
    )


def solution(mesh):
    placed = (P("rep", None, "lon", None), P(), P(), P(), P(), P(("rep", "lon"), None, None))
    return jax.shard_map(
        functools.partial(local, mesh.shape["lon"], mesh.shape["rep"]),
        mesh=mesh,
        in_specs=placed,
        out_specs=(P(("rep", "lon"), None, None), P("rep", None, "lon", None), P(), P(), P(), P()),
        check_vma=False,
    )
```

```python
import functools

import jax
import jax.numpy as jnp
from jax import lax
from jax.experimental import pallas as pl
from jax.experimental.pallas import tpu as pltpu
from jax.sharding import PartitionSpec as P

MESH = pl.DeviceIdType.MESH
F32 = jnp.float32
BF16 = jnp.bfloat16
C_IN, C_WIDE, C1, C2 = 24, 32, 32, 64


def grid_of(rows, cols):
    return (
        lax.broadcasted_iota(jnp.int32, (rows, cols), 0),
        lax.broadcasted_iota(jnp.int32, (rows, cols), 1),
    )


def ones_where(hit):
    return jnp.where(hit, 1.0, 0.0).astype(BF16)


def stem_pick():
    r, c = grid_of(256, 512)
    return ones_where(r == 2 * (c & 127) + (c >> 7) - 1)


def slab_order(width):
    r, c = grid_of(width * C_WIDE, C_IN * width)
    channel = r & (C_WIDE - 1)
    return ones_where((c == channel * width + (r >> 5)) & (channel < C_IN))


def mid_pick():
    r, c = grid_of(256, 384)
    return ones_where(((r >> 7) == ((c >> 6) & 1)) & ((r & 127) == 2 * (c & 63) + (c >> 7) - 1))


def mid_spread():
    r, c = grid_of(128, 768)
    return ones_where(
        ((r >> 6) == ((c >> 7) & 1)) & ((c & 127) == 2 * (r & 63) + (c >> 8) - 1)
    )


def stem_order(ah):
    r, c = grid_of(C_IN * 16, 256)
    return ones_where(r == (c & 31) * 16 + (2 * ah + (c >> 7)) * 4 + ((c >> 5) & 3))


def stem_rows():
    r, c = grid_of(C_IN * 16, 128)
    return ones_where(c == (r & 3) * C_WIDE + (r >> 4))


def dot(a, b, dims=((1,), (0,))):
    return lax.dot_general(a, b, (dims, ((), ())), preferred_element_type=F32)


def sigmoid(v):
    return 0.5 + 0.5 * jnp.tanh(0.5 * v)


def slope_of(v, g):
    return g * (1.0 + v * (1.0 - g))


def swapped(tile):
    return pltpu.roll(tile, 64, axis=1)


def lon_shift(x, step):
    if step == 0:
        return x
    if step == 1:
        return jnp.concatenate([x[:, 128:], swapped(x[:, :128])], axis=1)
    return jnp.concatenate([swapped(x[:, -128:]), x[:, :-128]], axis=1)


def lat_shift(x, step):
    if step == 0:
        return x
    n = x.shape[1]
    lat = lax.broadcasted_iota(jnp.int32, x.shape, 1) & 63
    if step == 1:
        return jnp.where(lat == 63, 0.0, pltpu.roll(x, n - 1, axis=1))
    return jnp.where(lat == 0, 0.0, pltpu.roll(x, 1, axis=1))


def kernel(
    nl, nr,
    fields, ws_hbm, wm_hbm, wh_hbm, ow_hbm, pc_hbm,
    pred, cot_out, all_a, all_b,
    ws, wm, wh, ow_in, pc_in,
    ws_all, wmb, pick_mid, spread_mid,
    got, e_buf, a_rows, f_buf, v_buf, m_rows, col_r, cc, cot_send,
    sum_a, half_a, one_a, mine_a, two_a,
    sum_b, half_b, one_b, mine_b, two_b,
    own_sem, w_sem, sf, rf, sc, rc,
    s1a, r1a, s2a, r2a, s3a, r3a,
    s1b, r1b, s2b, r2b, s3b, r3b,
):
    me, rep = lax.axis_index("lon"), lax.axis_index("rep")
    width = fields.shape[1] // C_IN
    per = width // 2
    lonh = nl * per
    hl = lonh // 2
    tiles = hl // 2

    def lon_peer(k):
        return (lax.rem(me + k, nl), rep)

    def rep_peer(k):
        return (me, lax.rem(rep + k, nr))

    def remote(src, dst, send, recv, peer):
        copy = pltpu.make_async_remote_copy(
            src_ref=src, dst_ref=dst, send_sem=send, recv_sem=recv,
            device_id=peer, device_id_type=MESH,
        )
        copy.start()
        return copy

    own = pltpu.make_async_copy(fields.at[me], got.at[me], own_sem.at[0])
    own.start()
    loads = []
    for i, (src, dst) in enumerate(((ws_hbm, ws), (wm_hbm, wm), (wh_hbm, wh), (ow_hbm, ow_in), (pc_hbm, pc_in))):
        load = pltpu.make_async_copy(src, dst, w_sem.at[i])
        load.start()
        loads.append(load)
    barrier = pltpu.get_barrier_semaphore()
    for k in range(1, nl):
        pl.semaphore_signal(barrier, inc=1, device_id=lon_peer(k), device_id_type=MESH)
    for k in range(1, nr):
        pl.semaphore_signal(barrier, inc=1, device_id=rep_peer(k), device_id_type=MESH)
    pl.semaphore_wait(barrier, nl - 1 + nr - 1)
    sends = []
    moved = []
    for k in range(1, nl):
        to = lax.rem(me + k, nl)
        moved.append(
            remote(fields.at[to], got.at[me], sf.at[k - 1], rf.at[k - 1], lon_peer(k))
        )
    sends += moved

    def spread_out(x, y, sums, halves, one, send, recv):
        x = jnp.concatenate([x, y], axis=1)
        pad = sums.shape[0] - x.shape[0]
        if pad:
            x = jnp.concatenate([x, jnp.zeros((pad, 128), F32)], axis=0)
        sums[...] = x
        halves[...] = x.astype(BF16)
        rows = sums.shape[0] // nl
        copies = []
        for k in range(1, nl):
            to = pl.ds(pl.multiple_of(lax.rem(me + k, nl) * rows, 16), rows)
            copies.append(
                remote(halves.at[to], one.at[k - 1], send.at[k - 1], recv.at[k - 1], lon_peer(k))
            )
        return copies

    def across(copies, sums, one, mine, two, send, recv):
        rows = sums.shape[0] // nl
        total = sums[pl.ds(pl.multiple_of(me * rows, 16), rows), :]
        for k in range(1, nl):
            copies[k - 1].wait_recv()
            total = total + one[k - 1].astype(F32)
        mine[...] = total.astype(BF16)
        out = []
        for k in range(1, nr):
            out.append(remote(mine, two.at[rep], send.at[k - 1], recv.at[k - 1], rep_peer(k)))
        two[rep] = mine[...]
        return out

    def gather(copies, two, everywhere, send, recv):
        rows = everywhere.shape[0] // nl
        for copy in copies:
            copy.wait_recv()
        total = two[0].astype(F32)
        for k in range(1, nr):
            total = total + two[k].astype(F32)
        here = pl.ds(pl.multiple_of(me * rows, 16), rows)
        everywhere[here, :] = total.astype(BF16)
        out = []
        for k in range(1, nl):
            out.append(
                remote(
                    everywhere.at[here], everywhere.at[here],
                    send.at[k - 1], recv.at[k - 1], lon_peer(k),
                )
            )
        return out

    for load in loads:
        load.wait()
    ws_rows = ws[...].astype(F32).reshape(C_IN * 16, C1).astype(BF16)
    for ah in range(2):
        ws_all[ah * C1 : (ah + 1) * C1, :] = dot(
            ws_rows, stem_order(ah), ((0,), (0,))
        ).astype(BF16)
    wide = wm[...].astype(F32)
    wmb[...] = jnp.concatenate(
        [
            jnp.concatenate(
                [wide[(a * 3 + b) * C1 : (a * 3 + b + 1) * C1] for a in range(3)], axis=0
            )
            for b in range(3)
        ],
        axis=1,
    ).astype(BF16)
    pick_mid[...] = mid_pick()
    spread_mid[...] = mid_spread()
    pick = stem_pick()
    order = slab_order(width)

    tall = width * C_WIDE
    for batch in (range(0, 1), range(1, nl // 2), range(nl // 2, nl)):
        for k in batch:
            if k == 0:
                own.wait()
            else:
                moved[k - 1].wait_recv()
        sources = [lax.rem(me - k + nl, nl) for k in batch]
        lines = [dot(order, got[source]).astype(BF16) for source in sources]
        taps = dot(jnp.concatenate(lines, axis=0), pick).astype(BF16)
        for at, source in enumerate(sources):
            for l in range(width):
                even = l % 2 == 0
                tile = source * per + l // 2 - (1 if even else 0)
                if l == 0:
                    tile = lax.rem(tile + lonh, lonh)
                where = pl.ds(pl.multiple_of(tile * 128, 128), 128)
                top = at * tall + l * C_WIDE
                for b in range(4):
                    row = (128 if even else 0) + b * C_WIDE
                    e_buf[row : row + C_WIDE, where] = taps[
                        top : top + C_WIDE, b * 128 : (b + 1) * 128
                    ]

    both = dot(ws_all[...], e_buf[...])
    last = (lonh - 1) * 128
    stem_pre = (
        jnp.concatenate([both[0:C1, last:], both[0:C1, :last]], axis=1) + both[C1:, :]
    )
    stem_g = sigmoid(stem_pre)
    stem_act = (stem_pre * stem_g).astype(BF16)
    stem_slope = slope_of(stem_pre, stem_g)

    for l in range(hl):
        a_rows[l * C1 : (l + 1) * C1, 0:128] = stem_act[:, l * 128 : (l + 1) * 128]
        a_rows[l * C1 : (l + 1) * C1, 128:256] = stem_act[:, (l + hl) * 128 : (l + hl + 1) * 128]
    u = dot(a_rows[...], pick_mid[...])
    ub = u.astype(BF16)
    for b in range(3):
        last = u[(hl - 1) * C1 : hl * C1, b * 128 : (b + 1) * 128]
        f_buf[b * C1 : (b + 1) * C1, 0:128] = swapped(last).astype(BF16)
        for l in range(hl):
            t = (l + 1) // 2
            row = (96 if l % 2 == 0 else 0) + b * C1
            f_buf[row : row + C1, t * 128 : (t + 1) * 128] = ub[
                l * C1 : (l + 1) * C1, b * 128 : (b + 1) * 128
            ]
    n = tiles * 128
    mid_pre = dot(wm[0:192, :], f_buf[:, 0:n], ((0,), (0,))) + dot(
        wm[192:288, :], f_buf[0:96, 128 : n + 128], ((0,), (0,))
    )
    mid_g = sigmoid(mid_pre)
    mid_act = (mid_pre * mid_g).astype(BF16)
    mid_slope = slope_of(mid_pre, mid_g)

    y = dot(wh[...], mid_act)
    head_pre = None
    for b in range(3):
        s = None
        for a in range(3):
            block = (a * 3 + b) * C2
            part = lon_shift(y[block : block + C2], a - 1)
            s = part if s is None else s + part
        s = lat_shift(s, b - 1)
        head_pre = s if head_pre is None else head_pre + s
    head_g = sigmoid(head_pre)
    head_act = (head_pre * head_g).astype(BF16).astype(F32)
    r, c = grid_of(C2, C2)
    ow = jnp.sum(jnp.where(r == c, ow_in[...], 0.0), axis=1, keepdims=True)
    pc = jnp.concatenate([pc_in[0:tiles, :], pc_in[tiles:, :]], axis=1)
    pc = jnp.concatenate([pc[t : t + 1, :] for t in range(tiles)], axis=1)
    pred[...] = jnp.sum(head_act * ow, axis=0, keepdims=True)
    out_sum = jnp.sum(head_act * pc, axis=1, keepdims=True)
    head_cot = (pc * ow * slope_of(head_pre, head_g)).astype(BF16).astype(F32)
    for b in range(3):
        moved_lat = lat_shift(head_cot, 1 - b)
        for a in range(3):
            block = (a * 3 + b) * C2
            col_r[block : block + C2, :] = lon_shift(moved_lat, 1 - a).astype(BF16)
    head_sum = dot(col_r[...], mid_act, ((1,), (1,)))
    mid_grad = dot(wh[...], col_r[...], ((0,), (0,))).astype(BF16).astype(F32)
    mid_cot = (mid_grad * mid_slope).astype(BF16)

    mid_sum_01 = dot(f_buf[:, 0:n], mid_cot, ((1,), (1,)))
    mid_sum_2 = dot(f_buf[0:96, 128 : n + 128], mid_cot, ((1,), (1,)))
    block_a = jnp.concatenate(
        [head_sum, jnp.broadcast_to(out_sum, (C2, C2)), mid_sum_01, mid_sum_2], axis=0
    )
    first_a = spread_out(block_a[:464], block_a[464:], sum_a, half_a, one_a, s1a, r1a)
    for t in range(tiles):
        m_rows[t * C2 : (t + 1) * C2, :] = mid_cot[:, t * 128 : (t + 1) * 128]
    up = dot(m_rows[...], spread_mid[...]).astype(BF16)
    for t in range(tiles):
        for b in range(3):
            for q in range(2):
                lon = t + q * tiles
                v_buf[b * C2 : (b + 1) * C2, lon * 128 : (lon + 1) * 128] = up[
                    t * C2 : (t + 1) * C2, b * 256 + q * 128 : b * 256 + (q + 1) * 128
                ]
    d = dot(wmb[...], v_buf[...])
    for i in range(lonh):
        m = i // 2
        if i % 2 == 0:
            grad = d[C1 : 2 * C1, m * 128 : (m + 1) * 128]
        else:
            nxt = (m + 1) % (lonh // 2)
            grad = d[2 * C1 :, m * 128 : (m + 1) * 128] + d[:C1, nxt * 128 : (nxt + 1) * 128]
        cot = grad.astype(BF16).astype(F32) * stem_slope[:, i * 128 : (i + 1) * 128]
        cot = cot.astype(BF16)
        before = (i - 1) % lonh
        cc[0:C1, before * 128 : (before + 1) * 128] = cot
        cc[C1 : 2 * C1, i * 128 : (i + 1) * 128] = cot
        cot_send[i // per, :, (i % per) * 128 : (i % per + 1) * 128] = cot
    second_a = across(first_a, sum_a, one_a, mine_a, two_a, s2a, r2a)
    stem_sum = dot(e_buf[...], cc[...], ((1,), (1,)))
    first_b = spread_out(stem_sum[:128], stem_sum[128:], sum_b, half_b, one_b, s1b, r1b)
    third_a = gather(second_a, two_a, all_a, s3a, r3a)
    back = []
    for k in range(1, nl):
        to = lax.rem(me + k, nl)
        back.append(
            remote(cot_send.at[to], cot_out.at[me], sc.at[k - 1], rc.at[k - 1], lon_peer(k))
        )
    own_back = pltpu.make_async_copy(cot_send.at[me], cot_out.at[me], own_sem.at[1])
    own_back.start()
    for copy in moved + first_a:
        copy.wait_send()
    second_b = across(first_b, sum_b, one_b, mine_b, two_b, s2b, r2b)
    for copy in second_a + third_a:
        copy.wait_send()
    third_b = gather(second_b, two_b, all_b, s3b, r3b)
    own_back.wait()
    for copy in first_b + second_b:
        copy.wait_send()
    for copy in third_a + back + third_b:
        copy.wait_recv()
    for copy in back + third_b:
        copy.wait_send()


def finish(factor, pred, cot, all_a, all_b, pred_out, cot_out, g_stem, g_mid, g_head, g_out):
    tiles = pred.shape[1] // 128
    lines = jnp.concatenate(
        [pred[:, t * 128 : (t + 1) * 128] for t in range(tiles)], axis=0
    )
    pred_out[0:tiles, :] = lines[:, 0:64]
    pred_out[tiles:, :] = lines[:, 64:128]
    a = all_a[0:464, :].astype(F32) * factor
    g_head[0:464, :] = a[:, 0:64]
    g_head[464:576, :] = a[0:112, 64:128]
    r, c = grid_of(C2, C2)
    g_out[...] = jnp.sum(
        jnp.where(r == c, a[112:176, 64:128], 0.0), axis=0, keepdims=True
    )
    g_mid[...] = a[176:464, 64:128]
    rows = dot(stem_rows(), all_b[0:128, :])
    r, c = grid_of(C_IN * 16, 128)
    group = (r >> 2) & 3
    kept = jnp.where((c >> 5) == (group & 1) * 2 + (group >> 1), rows, 0.0).astype(BF16)
    r, c = grid_of(128, C1)
    stem = dot(kept, ones_where((r & 31) == c)) * factor
    g_stem[...] = stem.reshape(g_stem.shape)
    for s in range(cot.shape[0]):
        whole = cot[s].astype(F32)
        cot_out[s] = whole.reshape(cot_out.shape[1:]).astype(BF16)


def local(nl, nr, fields, stem_weight, mid_weight, head_weight, out_weight, pred_cotangent):
    scen_here, _, width, lat = fields.shape
    per = width // 2
    lonh = nl * per
    tiles = lonh // 4
    lonc = 2 * tiles
    ws = stem_weight.transpose(1, 2, 3, 0).reshape(C_IN * 4, 4, C1)
    wm = mid_weight.transpose(2, 3, 1, 0).reshape(288, C2)
    wh = head_weight.transpose(2, 3, 0, 1).reshape(576, C2)
    vmem = pl.BlockSpec(memory_space=pltpu.VMEM)
    hbm = pl.BlockSpec(memory_space=pltpu.HBM)
    dma = pltpu.SemaphoreType.DMA

    def sum_scratch(size):
        return [
            pltpu.VMEM((size, 128), F32),
            pltpu.VMEM((size, 128), BF16),
            pltpu.VMEM((nl - 1, size // nl, 128), BF16),
            pltpu.VMEM((size // nl, 128), BF16),
            pltpu.VMEM((nr, size // nl, 128), BF16),
        ]

    sum_sems = [
        dma((nl - 1,)), dma((nl - 1,)),
        dma((nr - 1,)), dma((nr - 1,)),
        dma((nl - 1,)), dma((nl - 1,)),
    ]
    size_a = -(-464 // (nl * 16)) * nl * 16
    size_b = -(-128 // (nl * 16)) * nl * 16
    pred, cot, all_a, all_b = pl.pallas_call(
        functools.partial(kernel, nl, nr),
        out_shape=[
            jax.ShapeDtypeStruct((1, tiles * 128), F32),
            jax.ShapeDtypeStruct((nl, C1, per * 128), BF16),
            jax.ShapeDtypeStruct((size_a, 128), BF16),
            jax.ShapeDtypeStruct((size_b, 128), BF16),
        ],
        in_specs=[hbm] * 6,
        out_specs=[vmem, hbm, vmem, vmem],
        scratch_shapes=[
            pltpu.VMEM(ws.shape, BF16),
            pltpu.VMEM(wm.shape, BF16),
            pltpu.VMEM(wh.shape, BF16),
            pltpu.VMEM((1, C2), F32),
            pltpu.VMEM((lonc, 64), F32),
            pltpu.VMEM((2 * C1, 256), BF16),
            pltpu.VMEM((96, 192), BF16),
            pltpu.VMEM((256, 384), BF16),
            pltpu.VMEM((128, 768), BF16),
            pltpu.VMEM((nl, C_IN * width, lat), BF16),
            pltpu.VMEM((256, lonh * 128), BF16),
            pltpu.VMEM((lonh // 2 * C1, 256), BF16),
            pltpu.VMEM((192, (tiles + 1) * 128), BF16),
            pltpu.VMEM((192, lonc * 128), BF16),
            pltpu.VMEM((tiles * C2, 128), BF16),
            pltpu.VMEM((576, tiles * 128), BF16),
            pltpu.VMEM((2 * C1, lonh * 128), BF16),
            pltpu.VMEM((nl, C1, per * 128), BF16),
        ]
        + sum_scratch(size_a)
        + sum_scratch(size_b)
        + [
            dma((2,)), dma((5,)),
            dma((nl - 1,)), dma((nl - 1,)),
            dma((nl - 1,)), dma((nl - 1,)),
        ]
        + sum_sems
        + sum_sems,
        compiler_params=pltpu.CompilerParams(
            collective_id=0, has_side_effects=True, vmem_limit_bytes=60 * 2**20
        ),
    )(
        fields.reshape(scen_here, C_IN * width, lat),
        ws, wm, wh, out_weight.reshape(1, C2), pred_cotangent.reshape(lonc, 64),
    )
    prediction, stem_cotangent, g_stem, g_mid, g_head, g_out = pl.pallas_call(
        functools.partial(finish, 1.0 / (scen_here * nr)),
        out_shape=[
            jax.ShapeDtypeStruct((lonc, 64), F32),
            jax.ShapeDtypeStruct((nl, C1, per, 128), BF16),
            jax.ShapeDtypeStruct((C_IN * 4, 4, C1), F32),
            jax.ShapeDtypeStruct((288, C2), F32),
            jax.ShapeDtypeStruct((576, C2), F32),
            jax.ShapeDtypeStruct((1, C2), F32),
        ],
        in_specs=[vmem] * 4,
        out_specs=[vmem] * 6,
        compiler_params=pltpu.CompilerParams(vmem_limit_bytes=60 * 2**20),
    )(pred, cot, all_a, all_b)
    grad_stem = g_stem.reshape(C_IN, 4, 4, C1).transpose(3, 0, 1, 2)
    grad_mid = g_mid.reshape(3, 3, C1, C2).transpose(3, 2, 0, 1)
    grad_head = g_head.reshape(3, 3, C2, C2).transpose(2, 3, 0, 1)
    return (
        prediction.reshape(1, lonc, 64), stem_cotangent,
        grad_stem, grad_mid, grad_head, g_out.reshape(C2),
    )


def solution(mesh):
    placed = (P("rep", None, "lon", None), P(), P(), P(), P(), P(("rep", "lon"), None, None))
    return jax.shard_map(
        functools.partial(local, mesh.shape["lon"], mesh.shape["rep"]),
        mesh=mesh,
        in_specs=placed,
        out_specs=(P(("rep", "lon"), None, None), P("rep", None, "lon", None), P(), P(), P(), P()),
        check_vma=False,
    )
```
